512 devices in a mesh: grp: 16 (over z_hi, x), seq: 32 (over y, z_lo, core).
Axes of the slice: x: 4, y: 4, z: 16 (z_hi: 4, z_lo: 4; z = z_hi * 4 + z_lo), core: 2. Of those that a mesh axis runs over, the one named last changes fastest.
Arguments:
- queries: bfloat16 [262144, 384], P(('grp', 'seq')), may hold values from -6 to 6
- keys: bfloat16 [262144, 384], P(('grp', 'seq')), may hold values from -6 to 6
- values: bfloat16 [262144, 384], P(('grp', 'seq')), may hold values from -6 to 6
- offsets: int32 [2, 6], replicated, may hold values from 0 to 127, as said below
- out_weight: bfloat16 [384, 768], replicated, may hold values from -1.1953125 to 1.1953125
Outputs:
- mixed: bfloat16 [262144, 768], P(('grp', 'seq'))
The draws below stay inside these ranges and needn't reach their ends.
Inputs may be any that keep to these rules, and one draw needn't show every extreme that they name: Row 0 holds offsets below 8, row 1 offsets below 128; in each row one head has offset 0 and another the row's largest allowed value.
All inputs are finite; a program needn't handle non-finite values.
Results may differ from the reference program's by a relative error of at most 0.0052.
Values may be sent and summed in bfloat16 or wider, within the bound.
A program may use at most 64 MiB of HBM per device.

```python
import math
import jax
import jax.numpy as jnp
from jax import lax

D = 768
HEADS = 6
HEAD_DIM = 64
KEEP = 2048
TOK_DEV = 512
HD = 384
TOKENS = 262144
R_NEAR = 8
R_FAR = 128
N_GRP = 16
N_SEQ = 32


def draw_queries(key, part):
    key = jax.random.fold_in(key, 11)
    base = 1.4 * jnp.clip(jax.random.normal(key, (TOKENS, HD), jnp.float32), -4.2, 4.2)
    return base.astype(jnp.bfloat16)


def draw_keys(key, part):
    key = jax.random.fold_in(key, 23)
    base = 1.4 * jnp.clip(jax.random.normal(key, (TOKENS, HD), jnp.float32), -4.2, 4.2)
    return base.astype(jnp.bfloat16)


def draw_offsets(key, part):
    key = jax.random.fold_in(key, 5)
    levels_out = []
    for level_id, dilation in ((0, R_NEAR), (1, R_FAR)):
        level_key = jax.random.fold_in(key, level_id)
        chosen = jax.random.randint(jax.random.fold_in(level_key, 1), (HEADS,), 0, dilation, dtype=jnp.int32)
        order = jax.random.permutation(jax.random.fold_in(level_key, 2), HEADS)
        chosen = chosen.at[order[0]].set(0).at[order[1]].set(dilation - 1)
        levels_out.append(chosen)
    return jnp.stack(levels_out).astype(jnp.int32)


def level_of(key, dims, cuts, low, top_value):
    factor_of = 1.0
    for dim, shards_of in cuts:
        draws = jax.random.uniform(jax.random.fold_in(jax.random.fold_in(key, 6), dim), (shards_of,), jnp.float32, low / len(cuts), top_value / len(cuts))
        factor_of = factor_of * jnp.repeat(jnp.exp(draws), dims[dim] // shards_of).reshape((-1,) + (1,) * (len(dims) - 1 - dim))
    return factor_of


def bell_draw(stream_key, dims, deviation, reach, cuts=(), kind=jnp.bfloat16):
    loudness = level_of(stream_key, dims, cuts, -0.22, 0.18) if cuts else 1.0
    entries = jax.random.normal(stream_key, dims, jnp.float32) * deviation * loudness
    return jnp.minimum(jnp.maximum(entries, -reach), reach).astype(kind)


def setup_inputs(seed: int = 0) -> dict:
    seeds = jax.random.split(jax.random.key(seed), 6)
    return {
        "queries": draw_queries(jax.random.fold_in(seeds[5], 71), 0),
        "keys": draw_keys(jax.random.fold_in(seeds[5], 71), 0),
        "values": bell_draw(seeds[2], (TOKENS, HD), 1.0, 6.0, ((0, 512),)),
        "offsets": draw_offsets(jax.random.fold_in(seeds[5], 71), 0),
        "out_weight": bell_draw(seeds[4], (HD, D), 0.2, 1.1953125),
    }


NEGATIVE = -1e+30

def pick_rows(source, dilation, shifts):
    lanes = jnp.arange(dilation, dtype=jnp.int32)
    chosen = jnp.repeat(lanes[:, None] == shifts[None, :], HEAD_DIM, axis=1)
    grouped = source.reshape(source.shape[0] // dilation, dilation, source.shape[1])
    return lax.optimization_barrier(jnp.sum(jnp.where(chosen[None], grouped, jnp.zeros((), source.dtype)), axis=1))

def spread_rows(source, dilation, shifts, filler, repeat_by):
    lanes = jnp.arange(dilation, dtype=jnp.int32)
    chosen = jnp.repeat(lanes[:, None] == shifts[None, :], repeat_by, axis=1)
    spread = jnp.where(chosen[None], source[:, None, :], filler)
    return spread.reshape(source.shape[0] * dilation, source.shape[1])

def attend(asks, keys_in, values_in, first):
    count_ask = asks.shape[0]
    count_key = keys_in.shape[0]
    head_count = asks.shape[1] // HEAD_DIM
    asks_f = asks.reshape(count_ask, head_count, HEAD_DIM).astype(jnp.float32)
    keys_f = keys_in.reshape(count_key, head_count, HEAD_DIM).astype(jnp.float32)
    values_f = values_in.reshape(count_key, head_count, HEAD_DIM).astype(jnp.float32)
    scores = jnp.einsum('qhe,khe->hqk', asks_f, keys_f) * (1.0 / math.sqrt(HEAD_DIM))
    allowed = jnp.arange(count_key, dtype=jnp.int32)[None, :] <= (first + jnp.arange(count_ask, dtype=jnp.int32))[:, None]
    scores = jnp.where(allowed[None], scores, NEGATIVE)
    highest = lax.optimization_barrier(jnp.max(scores, axis=-1))
    weights = jnp.where(allowed[None], jnp.exp(scores - highest[..., None]), 0.0)
    totals = lax.optimization_barrier(jnp.sum(weights, axis=-1))
    rounded = lax.optimization_barrier(weights.astype(jnp.bfloat16)).astype(jnp.float32)
    summed = jnp.einsum('hqk,khe->qhe', rounded, values_f)
    output = (summed / totals.T[:, :, None]).reshape(count_ask, head_count * HEAD_DIM)
    return (output, (highest + jnp.log(totals)).T)

def merge_levels(outputs, spreads):
    highest = jnp.maximum(jnp.maximum(spreads[0], spreads[1]), spreads[2])
    shares = [jnp.exp(item - highest) for item in spreads]
    numer = jnp.repeat(shares[0], HEAD_DIM, axis=1) * outputs[0]
    numer = numer + jnp.repeat(shares[1], HEAD_DIM, axis=1) * outputs[1]
    numer = numer + jnp.repeat(shares[2], HEAD_DIM, axis=1) * outputs[2]
    denom = shares[0] + shares[1] + shares[2]
    return (numer / jnp.repeat(denom, HEAD_DIM, axis=1)).astype(jnp.bfloat16)

def reference(queries, keys, values, offsets, out_weight):
    far_shift = offsets[1]
    near_shift = offsets[0]
    far_out, far_lse = attend(pick_rows(queries, R_FAR, far_shift), pick_rows(keys, R_FAR, far_shift), pick_rows(values, R_FAR, far_shift), 0)
    group_len = TOK_DEV * N_SEQ

    def one_group(bundle):
        group_q, group_k, group_v, far_o, far_l = bundle
        near_out, near_lse = attend(pick_rows(group_q, R_NEAR, near_shift), pick_rows(group_k, R_NEAR, near_shift), pick_rows(group_v, R_NEAR, near_shift), 0)

        def one_device(pieces):
            return attend(pieces[0], pieces[1], pieces[2], 0)
        local_out, local_lse = lax.map(one_device, (group_q.reshape(N_SEQ, TOK_DEV, HD), group_k.reshape(N_SEQ, TOK_DEV, HD), group_v.reshape(N_SEQ, TOK_DEV, HD)))
        local_out = local_out.reshape(group_len, HD)
        local_lse = local_lse.reshape(group_len, HEADS)
        outputs = [local_out, spread_rows(near_out, R_NEAR, near_shift, 0.0, HEAD_DIM), spread_rows(far_o, R_FAR, far_shift, 0.0, HEAD_DIM)]
        spreads = [local_lse, spread_rows(near_lse, R_NEAR, near_shift, NEGATIVE, 1), spread_rows(far_l, R_FAR, far_shift, NEGATIVE, 1)]
        merged = merge_levels(outputs, spreads)
        return jnp.dot(merged, out_weight, preferred_element_type=jnp.float32).astype(jnp.bfloat16)
    result = lax.map(one_group, (queries.reshape(N_GRP, group_len, HD), keys.reshape(N_GRP, group_len, HD), values.reshape(N_GRP, group_len, HD), far_out.reshape(N_GRP, KEEP // N_GRP, HD), far_lse.reshape(N_GRP, KEEP // N_GRP, HEADS)))
    return result.reshape(TOKENS, D)
```

```python
import functools
import math

import jax
import jax.numpy as jnp
from jax import lax
from jax.experimental import pallas as pl
from jax.experimental.pallas import tpu as pltpu
from jax.sharding import PartitionSpec as P

MESH = pl.DeviceIdType.MESH
HEADS = 6
HD = 64
TOK = 512
SEQ = 32
GRP = 16
NEG = -1e30
C = math.log2(math.e) / math.sqrt(HD)
F32 = jnp.float32
BF16 = jnp.bfloat16


def nt(a, b):
    return lax.dot_general(a, b, (((1,), (1,)), ((), ())), preferred_element_type=F32)


def nn(a, b):
    return lax.dot_general(a, b, (((1,), (0,)), ((), ())), preferred_element_type=F32)


def tn(a, b):
    return lax.dot_general(a, b, (((0,), (0,)), ((), ())), preferred_element_type=F32)


def iota(shape, dim):
    return lax.broadcasted_iota(jnp.int32, shape, dim)


def onehot(cond):
    return jnp.where(cond, 1.0, 0.0).astype(BF16)


def near_chip(h):
    return (5 * h + 1) % 16


def far_chip(h):
    return (5 * (h + 6) + 1) % 16


def three(x):
    hi = x.astype(BF16).astype(F32)
    rest = x - hi
    mid = rest.astype(BF16).astype(F32)
    return hi, mid, rest - mid


def kernel(
    q_ref, k_ref, v_ref, off_ref, out_ref,
    kv_send, q_send, f_send, kv_in, q_in, f_in, qz, kvt, scr, ret_send, ret_in,
    kvx, fret_send, fret_in, acc, top, tot,
    kv_ss, q_ss, f_ss, kv_rs, q_rs, f_rs, x_ss, x_rs, ret_ss, ret_rs, fret_ss, fret_rs,
):
    s = lax.axis_index("seq")
    g = lax.axis_index("grp")
    chip, core = s // 2, s % 2
    role = ((chip + 15) * 13) % 16
    is_near = role < HEADS
    is_far = (role >= HEADS) & (role < 2 * HEADS) & (core == 0)
    head = role % HEADS
    is_worker = is_near | is_far

    barrier = pltpu.get_barrier_semaphore()

    def hello(target):
        pl.semaphore_signal(barrier, inc=1, device_id={"seq": target}, device_id_type=MESH)

    @pl.when(is_worker)
    def _():
        def step(i, _):
            @pl.when(i != s)
            def _():
                hello(i)
            return 0
        lax.fori_loop(0, SEQ, step, 0)

    @pl.when(jnp.logical_not(is_worker))
    def _():
        for h in range(HEADS):
            hello(2 * far_chip(h))
            hello(2 * near_chip(h))
            hello(2 * near_chip(h) + 1)

    @pl.when(is_far)
    def _():
        def step(i, _):
            pl.semaphore_signal(barrier, inc=1, device_id={"grp": i}, device_id_type=MESH)
            return 0
        lax.fori_loop(0, g, step, 0)

    lane = iota((32, 128), 1)
    low = lane < HD
    low16 = iota((16, 128), 1) < HD
    row16 = iota((16, 128), 0)
    near_diff = iota((32, 256), 1) - 8 * iota((32, 256), 0)
    fr = iota((16, TOK), 0)
    far_diff = jnp.where(fr < 8, iota((16, TOK), 1) - 128 * (fr % 4), -1)

    def turn(x):
        return pltpu.roll(x, HD, 1)

    for p in range(3):
        near_hot = [onehot(near_diff == off_ref[0, 2 * p + e]) for e in range(2)]
        far_hot = [onehot(far_diff == off_ref[1, 2 * p + e]) for e in range(2)]
        picked = []
        for ref in (q_ref, k_ref, v_ref):
            halves = []
            for a in range(2):
                left = jnp.concatenate(near_hot + [f[:, 256 * a:256 * a + 256] for f in far_hot], axis=0)
                halves.append(nn(left, ref[256 * a:256 * a + 256, 128 * p:128 * p + 128]))
            picked.append(halves)
        pq, pk, pv = picked
        for e in range(2):
            h = 2 * p + e
            for a in range(2):
                rk, rv = pk[a][32 * e:32 * e + 32], pv[a][32 * e:32 * e + 32]
                kv = jnp.where(low, rk, turn(rv)) if e == 0 else jnp.where(low, turn(rk), rv)
                kv_send[h, 32 * a:32 * a + 32, :] = kv.astype(BF16)
            r0, r1 = pq[0][32 * e:32 * e + 32], pq[1][32 * e:32 * e + 32]
            qq = jnp.where(low, r0, turn(r1)) if e == 0 else jnp.where(low, turn(r0), r1)
            q_send[h] = qq.astype(BF16)
            lo = 64 + 16 * e
            fq, fk, fv = [x[0][lo:lo + 16] + x[1][lo:lo + 16] for x in (pq, pk, pv)]
            if e == 0:
                fkv, fqz = jnp.where(low16, fk, turn(fv)), fq
            else:
                fkv, fqz = jnp.where(low16, turn(fk), fv), turn(fq)
            tile = jnp.where(row16 < 4, fkv, jnp.where(low16 & (row16 < 8), fqz, 0.0))
            f_send[h] = tile.astype(BF16)

    @pl.when(is_far)
    def _():
        pl.semaphore_wait(barrier, SEQ - 1 + GRP - 1 - g)

    @pl.when(is_near)
    def _():
        pl.semaphore_wait(barrier, SEQ - 1)

    @pl.when(jnp.logical_not(is_worker))
    def _():
        pl.semaphore_wait(barrier, 3 * HEADS)

    def copy(src, dst, ss, rs, target):
        return pltpu.make_async_remote_copy(
            src_ref=src, dst_ref=dst, send_sem=ss, recv_sem=rs, device_id={"seq": target}, device_id_type=MESH
        )

    def send(src, dst, ss, rs, target):
        @pl.when(s == target)
        def _():
            pltpu.make_async_copy(src, dst, rs).start()

        @pl.when(s != target)
        def _():
            copy(src, dst, ss, rs, target).start()

    def sent(src, dst, ss, rs, target):
        @pl.when(s != target)
        def _():
            copy(src, dst, ss, rs, target).wait_send()

    def slot(n, i):
        return pl.ds(pl.multiple_of(n * i, n), n)

    def outgoing(f):
        for h in range(HEADS):
            f(f_send.at[h], f_in.at[slot(16, s)], f_ss.at[h], f_rs.at[s], 2 * far_chip(h))
        for h in range(HEADS):
            for c in range(2):
                f(kv_send.at[h], kv_in.at[slot(64, s)], kv_ss.at[h, c], kv_rs.at[s], 2 * near_chip(h) + c)
            f(q_send.at[h], q_in.at[slot(32, chip)], q_ss.at[h], q_rs.at[chip], 2 * near_chip(h) + core)

    outgoing(send)

    eye = onehot(iota((128, 128), 0) == iota((128, 128), 1))
    causal = iota((256, 256), 0) <= iota((256, 256), 1)
    lane_q = iota((TOK, 128), 1) < HD
    row_v = iota((128, TOK), 0) < HD

    def local_pair(p):
        cols = slice(128 * p, 128 * p + 128)
        kp, qp, vp = k_ref[:, cols], q_ref[:, cols], v_ref[:, cols]
        vt = nt(eye, vp)
        for e in range(2):
            h = 2 * p + e
            mine = lane_q if e == 0 else jnp.logical_not(lane_q)
            qe = jnp.where(mine, qp, jnp.zeros((), BF16))
            mine_v = row_v if e == 0 else jnp.logical_not(row_v)
            ve = jnp.where(mine_v, vt, 1.0).astype(BF16)
            for t in range(2):
                qt = qe[256 * t:256 * t + 256]
                parts = [nt(kp[256 * b:256 * b + 256], qt) for b in range(t + 1)]
                parts[t] = jnp.where(causal, parts[t], NEG)
                m = jnp.max(parts[0], axis=0, keepdims=True)
                for x in parts[1:]:
                    m = jnp.maximum(m, jnp.max(x, axis=0, keepdims=True))
                o = None
                for b, x in enumerate(parts):
                    w = jnp.exp2((x - m) * C).astype(BF16)
                    y = nn(ve[:, 256 * b:256 * b + 256], w)
                    o = y if o is None else o + y
                ts = slice(256 * t, 256 * t + 256)
                acc[64 * h:64 * h + 64, ts] = o[64 * e:64 * e + 64]
                other = 64 * (1 - e)
                tot[h, :, ts] = o[other:other + 1]
                top[h, :, ts] = m * C

    local_pair(0)

    @pl.when(is_far)
    def _():
        def wait(i, _):
            copy(f_in.at[slot(16, i)], f_in.at[slot(16, i)], f_ss.at[0], f_rs.at[i], 0).wait_recv()
            return 0
        lax.fori_loop(0, SEQ, wait, 0)
        i, j = iota((128, TOK), 0), iota((128, TOK), 1)
        base = 16 * (i // 4) + i % 4
        rows = f_in[...]
        kvx[slot(128, g), :] = nn(onehot(j == base), rows).astype(BF16)
        qz[0:128, :] = nn(onehot(j == base + 4), rows).astype(BF16)

        def start(i, _):
            pltpu.make_async_remote_copy(
                src_ref=kvx.at[slot(128, g)], dst_ref=kvx.at[slot(128, g)], send_sem=x_ss.at[i],
                recv_sem=x_rs.at[g], device_id={"grp": i}, device_id_type=MESH,
            ).start()
            return 0
        lax.fori_loop(g + 1, GRP, start, 0)

        def clear(i, _):
            kvx[slot(128, i), :] = jnp.zeros((128, 128), BF16)
            return 0
        lax.fori_loop(g + 1, GRP, clear, 0)

    local_pair(1)
    local_pair(2)

    row_one = iota((128, TOK), 0) < HD
    low1 = iota((1, 128), 1) < HD

    @pl.when(is_near)
    def _():
        def wait(i, _):
            copy(kv_in.at[slot(64, i)], kv_in.at[slot(64, i)], q_ss.at[0], kv_rs.at[i], 0).wait_recv()
            return 0
        lax.fori_loop(0, SEQ, wait, 0)

        def wait_q(i, _):
            copy(q_in.at[slot(32, i)], q_in.at[slot(32, i)], q_ss.at[0], q_rs.at[i], 0).wait_recv()
            return 0
        lax.fori_loop(0, 16, wait_q, 0)
        for j in range(16):
            x = q_in[32 * j:32 * j + 32, :].astype(F32)
            qz[64 * j:64 * j + 32, :] = jnp.where(low, x, 0.0).astype(BF16)
            qz[64 * j + 32:64 * j + 64, :] = jnp.where(low, turn(x), 0.0).astype(BF16)
        for b in range(4):
            x = nt(eye, kv_in[TOK * b:TOK * b + TOK, :])
            kvt[:, TOK * b:TOK * b + TOK] = jnp.where(row_one, 1.0, x).astype(BF16)
        ask = iota((TOK, 256), 1)
        ask = (ask // 64) * 128 + core * 64 + ask % 64
        allowed = iota((TOK, 256), 0) <= ask
        for t in range(4):
            qt = qz[256 * t:256 * t + 256, :]
            m = None
            for b in range(t + 1):
                x = nt(kv_in[TOK * b:TOK * b + TOK, :], qt)
                if b == t:
                    x = jnp.where(allowed, x, NEG)
                scr[TOK * b:TOK * b + TOK, :] = x
                y = jnp.max(x, axis=0, keepdims=True)
                m = y if m is None else jnp.maximum(m, y)
            o = None
            for b in range(t + 1):
                w = jnp.exp2((scr[TOK * b:TOK * b + TOK, :] - m) * C).astype(BF16)
                y = nn(kvt[:, TOK * b:TOK * b + TOK], w)
                o = y if o is None else o + y
            total = o[0:1]
            norm = o[64:128] / total
            lses = three(m * C + jnp.log(total) * math.log2(math.e))
            for jj in range(4):
                j = 4 * t + jj
                cols = slice(128 * (jj // 2), 128 * (jj // 2) + 128)
                top_half, bottom = norm[0:32, cols], norm[32:64, cols]
                ls = [x[:, cols] for x in lses]
                if jj % 2 == 0:
                    packed = jnp.where(low, top_half, turn(bottom))
                else:
                    packed = jnp.where(low, turn(top_half), bottom)
                tail = jnp.where(row16 == 0, ls[0], jnp.where(row16 == 1, ls[1], jnp.where(row16 == 2, ls[2], 0.0)))
                if jj % 2 == 1:
                    tail = turn(tail)
                ret_send[j, 0:32, :] = packed.astype(BF16)
                ret_send[j, 32:48, :] = tail.astype(BF16)
                send(ret_send.at[j], ret_in.at[head], ret_ss.at[j], ret_rs.at[head], 2 * j + core)

    @pl.when(is_far)
    def _():
        def wait(i, _):
            pltpu.make_async_remote_copy(
                src_ref=kvx.at[slot(128, i)], dst_ref=kvx.at[slot(128, i)], send_sem=x_ss.at[i],
                recv_sem=x_rs.at[i], device_id={"grp": i}, device_id_type=MESH,
            ).wait_recv()
            return 0
        lax.fori_loop(0, g, wait, 0)
        qf = qz[0:128, :]
        limit = iota((TOK, 128), 1) + 128 * g
        m = None
        for b in range(4):
            x = nt(kvx[TOK * b:TOK * b + TOK, :], qf)
            x = jnp.where(iota((TOK, 128), 0) + TOK * b <= limit, x, NEG)
            scr[TOK * b:TOK * b + TOK, 0:128] = x
            y = jnp.max(x, axis=0, keepdims=True)
            m = y if m is None else jnp.maximum(m, y)
        o = None
        for b in range(4):
            xt = nt(eye, kvx[TOK * b:TOK * b + TOK, :])
            xt = jnp.where(row_one, 1.0, xt).astype(BF16)
            w = jnp.exp2((scr[TOK * b:TOK * b + TOK, 0:128] - m) * C).astype(BF16)
            y = nn(xt, w)
            o = y if o is None else o + y
        total = o[0:1]
        norm = (o[64:128] / total).astype(BF16)
        ls = three(m * C + jnp.log(total) * math.log2(math.e))
        r = iota((64, 128), 0)
        tail = jnp.where(r == 0, ls[0], jnp.where(r == 1, ls[1], jnp.where(r == 2, ls[2], 0.0)))
        both = jnp.concatenate([norm, tail.astype(BF16)], axis=0)
        i, j = iota((TOK, 128), 0), iota((TOK, 128), 1)
        place = onehot((j == 4 * (i // 16) + i % 16) & (i % 16 < 4))
        fret_send[...] = nt(place, both).astype(BF16)

        def start(i, _):
            send(fret_send.at[slot(16, i)], fret_in.at[head], fret_ss.at[i], fret_rs.at[head], i)
            return 0
        lax.fori_loop(0, SEQ, start, 0)

    spread = iota((128, TOK), 1) - 8 * (iota((128, TOK), 0) % 64)
    tok = iota((1, TOK), 1)
    low48 = iota((48, 128), 1) < HD
    for h in range(HEADS):
        copy(ret_in.at[h], ret_in.at[h], ret_ss.at[0], ret_rs.at[h], 0).wait_recv()
        near_off, far_off = off_ref[0, h], off_ref[1, h]
        x = ret_in[h]
        zero = jnp.zeros((), BF16)
        left = jnp.concatenate([jnp.where(low48, x, zero), jnp.where(low, zero, x[0:32])], axis=0)
        u = nn(left, onehot(spread == near_off))
        l1 = jnp.where(tok % 8 == near_off, u[32:33] + u[33:34] + u[34:35], NEG)
        copy(fret_in.at[h], fret_in.at[h], fret_ss.at[0], fret_rs.at[h], 0).wait_recv()
        w = tn(fret_in[h], onehot(far_diff == far_off))
        l2 = jnp.where(tok % 128 == far_off, w[64:65] + w[65:66] + w[66:67], NEG)
        m0 = top[h]
        big = jnp.maximum(jnp.maximum(m0, l1), l2)
        w0, w1, w2 = jnp.exp2(m0 - big), jnp.exp2(l1 - big), jnp.exp2(l2 - big)
        inv = 1.0 / (w0 * tot[h] + w1 + w2)
        w0, w1, w2 = w0 * inv, w1 * inv, w2 * inv
        for a in range(2):
            rows = slice(64 * h + 32 * a, 64 * h + 32 * a + 32)
            n1 = u[48 * a:48 * a + 32]
            n2 = w[32 * a:32 * a + 32]
            out_ref[rows, :] = (acc[rows, :] * w0 + n1 * w1 + n2 * w2).astype(BF16)

    outgoing(sent)

    @pl.when(is_near)
    def _():
        def step(j, _):
            sent(ret_send.at[j], ret_in.at[head], ret_ss.at[j], ret_rs.at[head], 2 * j + core)
            return 0
        lax.fori_loop(0, 16, step, 0)

    @pl.when(is_far)
    def _():
        def step(i, _):
            sent(fret_send.at[slot(16, i)], fret_in.at[head], fret_ss.at[i], fret_rs.at[head], i)
            return 0
        lax.fori_loop(0, SEQ, step, 0)

        def step_x(i, _):
            pltpu.make_async_remote_copy(
                src_ref=kvx.at[slot(128, g)], dst_ref=kvx.at[slot(128, g)], send_sem=x_ss.at[i],
                recv_sem=x_rs.at[g], device_id={"grp": i}, device_id_type=MESH,
            ).wait_send()
            return 0
        lax.fori_loop(g + 1, GRP, step_x, 0)


def on_device(queries, keys, values, offsets, out_weight):
    vm = pl.BlockSpec(memory_space=pltpu.VMEM)
    dma = pltpu.SemaphoreType.DMA
    merged = pl.pallas_call(
        kernel,
        out_shape=jax.ShapeDtypeStruct((HEADS * HD, TOK), BF16),
        in_specs=[vm, vm, vm, pl.BlockSpec(memory_space=pltpu.SMEM)],
        out_specs=vm,
        scratch_shapes=[
            pltpu.VMEM((HEADS, 64, 128), BF16),
            pltpu.VMEM((HEADS, 32, 128), BF16),
            pltpu.VMEM((HEADS, 16, 128), BF16),
            pltpu.VMEM((2048, 128), BF16),
            pltpu.VMEM((512, 128), BF16),
            pltpu.VMEM((512, 128), BF16),
            pltpu.VMEM((1024, 128), BF16),
            pltpu.VMEM((128, 2048), BF16),
            pltpu.VMEM((2048, 256), F32),
            pltpu.VMEM((16, 48, 128), BF16),
            pltpu.VMEM((HEADS, 48, 128), BF16),
            pltpu.VMEM((2048, 128), BF16),
            pltpu.VMEM((512, 128), BF16),
            pltpu.VMEM((HEADS, 16, 128), BF16),
            pltpu.VMEM((HEADS * HD, TOK), F32),
            pltpu.VMEM((HEADS, 1, TOK), F32),
            pltpu.VMEM((HEADS, 1, TOK), F32),
            dma((HEADS, 2)), dma((HEADS,)), dma((HEADS,)),
            dma((SEQ,)), dma((16,)), dma((SEQ,)),
            dma((GRP,)), dma((GRP,)),
            dma((16,)), dma((HEADS,)),
            dma((SEQ,)), dma((HEADS,)),
        ],
        compiler_params=pltpu.CompilerParams(
            collective_id=0, has_side_effects=True, vmem_limit_bytes=48 * 1024 * 1024
        ),
    )(queries, keys, values, offsets)
    return tn(merged, out_weight).astype(BF16)


def solution(mesh):
    placed = (P(("grp", "seq"), None), P(("grp", "seq"), None), P(("grp", "seq"), None), P(), P())
    return jax.shard_map(
        on_device, mesh=mesh, in_specs=placed, out_specs=P(("grp", "seq"), None), check_vma=False
    )
```

```python
import math

import jax
import jax.numpy as jnp
from jax import lax
from jax.experimental import pallas as pl
from jax.experimental.pallas import tpu as pltpu
from jax.sharding import PartitionSpec as P

MESH = pl.DeviceIdType.MESH
HEADS = 6
HD = 64
TOK = 512
SEQ = 32
GRP = 16
NEG = -1e30
C = math.log2(math.e) / math.sqrt(HD)
F32 = jnp.float32
BF16 = jnp.bfloat16


def nt(a, b):
    return lax.dot_general(a, b, (((1,), (1,)), ((), ())), preferred_element_type=F32)


def nn(a, b):
    return lax.dot_general(a, b, (((1,), (0,)), ((), ())), preferred_element_type=F32)


def tn(a, b):
    return lax.dot_general(a, b, (((0,), (0,)), ((), ())), preferred_element_type=F32)


def iota(shape, dim):
    return lax.broadcasted_iota(jnp.int32, shape, dim)


def onehot(cond):
    return jnp.where(cond, 1.0, 0.0).astype(BF16)


def near_chip(h):
    return (5 * h + 1) % 16


def far_chip(h):
    return (5 * (h + 6) + 1) % 16


def turn(x):
    return pltpu.roll(x, HD, 1)


def three(x):
    hi = x.astype(BF16).astype(F32)
    rest = x - hi
    mid = rest.astype(BF16).astype(F32)
    return hi, mid, rest - mid


def loop(lo, hi, f):
    def step(i, c):
        f(i)
        return c

    lax.fori_loop(lo, hi, step, 0)


def kernel(
    q_hbm, k_hbm, v_hbm, off_hbm, out_ref,
    q_ref, k_ref, v_ref, off_ref,
    n_send, f_send, n_in, o_in, f_in, qz, kvt, scr, ret_send, ret_in,
    kvx, fret_send, fret_in, acc, top, tot, spread, far_hot,
    in_sem, out_ss, n_rs, o_rs, f_rs, z_ss, x_ss, fw_ss, blk_rs, go, ret_ss, ret_rs, fret_rs,
):
    s = lax.axis_index("seq")
    g = lax.axis_index("grp")
    chip, core = s // 2, s % 2
    zh, gx = g // 4, g % 4
    role = ((chip + 15) * 13) % 16
    is_near = role < HEADS
    on_far = (role >= HEADS) & (role < 2 * HEADS)
    is_far = on_far & (core == 0)
    head = role % HEADS
    sibling = s + 1 - 2 * core

    inputs = [
        pltpu.make_async_copy(src, dst, in_sem.at[i])
        for i, (src, dst) in enumerate(
            ((off_hbm, off_ref), (q_hbm, q_ref), (k_hbm, k_ref), (v_hbm, v_ref))
        )
    ]
    for c in inputs:
        c.start()

    barrier = pltpu.get_barrier_semaphore()

    def hello(axis, target):
        pl.semaphore_signal(barrier, inc=1, device_id={axis: target}, device_id_type=MESH)

    @pl.when(is_near | is_far)
    def _():
        def step(i):
            part = ((i // 2 + 15) * 13) % 16
            skip = (part >= HEADS) & (part < 2 * HEADS) & (i % 2 == 0)

            @pl.when((i != s) & jnp.logical_not(skip))
            def _():
                hello("seq", i)
        loop(0, SEQ, step)

    @pl.when(is_far)
    def _():
        for i in range(1, 4):
            hello("grp", 4 * zh + (gx + i) % 4)
        loop(0, zh, lambda z: hello("grp", 4 * z + gx))

    low = iota((32, 128), 1) < HD
    low16 = iota((16, 128), 1) < HD
    row16 = iota((16, 128), 0)
    near_diff = iota((32, 256), 1) - 8 * iota((32, 256), 0)
    fr = iota((16, TOK), 0)
    far_diff = jnp.where(fr < 8, iota((16, TOK), 1) - 128 * (fr % 4), -1)
    for c in inputs:
        c.wait()
    for p in range(3):
        near_hot = [onehot(near_diff == off_ref[0, 2 * p + e]) for e in range(2)]
        hot = [onehot(far_diff == off_ref[1, 2 * p + e]) for e in range(2)]
        for e in range(2):
            far_hot[2 * p + e] = hot[e]
        picked = []
        for ref in (q_ref, k_ref, v_ref):
            halves = []
            for a in range(2):
                left = jnp.concatenate(near_hot + [f[:, 256 * a:256 * a + 256] for f in hot], axis=0)
                halves.append(nn(left, ref[256 * a:256 * a + 256, 128 * p:128 * p + 128]))
            picked.append(halves)
        pq, pk, pv = picked
        for e in range(2):
            h = 2 * p + e
            for a in range(2):
                rk, rv = pk[a][32 * e:32 * e + 32], pv[a][32 * e:32 * e + 32]
                kv = jnp.where(low, rk, turn(rv)) if e == 0 else jnp.where(low, turn(rk), rv)
                n_send[h, 32 * a:32 * a + 32, :] = kv.astype(BF16)
            r0, r1 = pq[0][32 * e:32 * e + 32], pq[1][32 * e:32 * e + 32]
            qq = jnp.where(low, r0, turn(r1)) if e == 0 else jnp.where(low, turn(r0), r1)
            n_send[h, 64:96, :] = qq.astype(BF16)
            lo = 64 + 16 * e
            fq, fk, fv = [x[0][lo:lo + 16] + x[1][lo:lo + 16] for x in (pq, pk, pv)]
            if e == 0:
                fkv, fqz = jnp.where(low16, fk, turn(fv)), fq
            else:
                fkv, fqz = jnp.where(low16, turn(fk), fv), turn(fq)
            tile = jnp.where(row16 < 4, fkv, jnp.where(low16 & (row16 < 8), fqz, 0.0))
            f_send[h] = tile.astype(BF16)

    @pl.when(is_near)
    def _():
        pl.semaphore_wait(barrier, 3 * HEADS - 1)

    @pl.when(jnp.logical_not(is_near | is_far))
    def _():
        pl.semaphore_wait(barrier, 3 * HEADS)

    @pl.when(on_far & (core == 1))
    def _():
        pl.semaphore_signal(go, inc=1, device_id={"seq": sibling}, device_id_type=MESH)

    @pl.when(is_far)
    def _():
        pl.semaphore_wait(go, 1)

    def copy(src, dst, ss, rs, target, axis="seq"):
        return pltpu.make_async_remote_copy(
            src_ref=src, dst_ref=dst, send_sem=ss, recv_sem=rs, device_id={axis: target}, device_id_type=MESH
        )

    def send(src, dst, ss, rs, target):
        @pl.when(s == target)
        def _():
            pltpu.make_async_copy(src, dst, rs).start()

        @pl.when(s != target)
        def _():
            copy(src, dst, ss, rs, target).start()

    def arrived(dst, rs):
        copy(dst, dst, in_sem.at[0], rs, sibling).wait_recv()

    def sent(src, ss):
        copy(src, src, ss, in_sem.at[0], sibling).wait_send()

    for i in range(HEADS):
        h = (chip + i) % HEADS
        send(f_send.at[h], f_in.at[s], out_ss.at[0], f_rs, 2 * far_chip(h))
    for i in range(HEADS):
        h = (chip + i) % HEADS
        send(n_send.at[h], n_in.at[chip], out_ss.at[1], n_rs.at[chip // 4], 2 * near_chip(h) + core)
    for i in range(HEADS):
        h = (chip + i) % HEADS
        copy(
            n_send.at[h, pl.ds(0, 64)], o_in.at[chip], out_ss.at[2], o_rs.at[chip // 4], 2 * near_chip(h) + 1 - core
        ).start()

    eye = onehot(iota((128, 128), 0) == iota((128, 128), 1))
    causal = iota((256, 256), 0) <= iota((256, 256), 1)
    lane_q = iota((TOK, 128), 1) < HD
    row_v = iota((128, TOK), 0) < HD
    row_one = iota((128, 256), 0) < HD

    def local_pair(p):
        cols = slice(128 * p, 128 * p + 128)
        kp, qp, vp = k_ref[:, cols], q_ref[:, cols], v_ref[:, cols]
        vt = nt(eye, vp)
        for e in range(2):
            h = 2 * p + e
            mine = lane_q if e == 0 else jnp.logical_not(lane_q)
            qe = jnp.where(mine, qp, jnp.zeros((), BF16))
            mine_v = row_v if e == 0 else jnp.logical_not(row_v)
            ve = jnp.where(mine_v, vt, 1.0).astype(BF16)
            for t in range(2):
                qt = qe[256 * t:256 * t + 256]
                parts = [nt(kp[256 * b:256 * b + 256], qt) for b in range(t + 1)]
                parts[t] = jnp.where(causal, parts[t], NEG)
                m = jnp.max(parts[0], axis=0, keepdims=True)
                for x in parts[1:]:
                    m = jnp.maximum(m, jnp.max(x, axis=0, keepdims=True))
                o = None
                for b, x in enumerate(parts):
                    w = jnp.exp2((x - m) * C).astype(BF16)
                    y = nn(ve[:, 256 * b:256 * b + 256], w)
                    o = y if o is None else o + y
                ts = slice(256 * t, 256 * t + 256)
                acc[64 * h:64 * h + 64, ts] = o[64 * e:64 * e + 64]
                other = 64 * (1 - e)
                tot[h, :, ts] = o[other:other + 1]
                top[h, :, ts] = m * C

    def to_z(z):
        return copy(kvx.at[g], kvx.at[g], z_ss.at[z], blk_rs.at[g], 4 * z + gx, "grp")

    def to_x(b, ss, x):
        return copy(kvx.at[b], kvx.at[b], ss, blk_rs.at[b], 4 * zh + x, "grp")

    for p in range(3):
        local_pair(p)

    @pl.when(is_far)
    def _():
        def clear(b):
            kvx[b] = jnp.zeros((128, 128), BF16)
        loop(g + 1, GRP, clear)
        arrived(f_in, f_rs)
        i, j = iota((128, TOK), 0), iota((128, TOK), 1)
        base = 16 * (i // 4) + i % 4
        rows = f_in[...].reshape(TOK, 128)
        kvx[g] = nn(onehot(j == base), rows).astype(BF16)
        qz[...] = nn(onehot(j == base + 4), rows).astype(BF16)
        pl.semaphore_wait(barrier, 6 - zh)
        loop(zh + 1, 4, lambda z: to_z(z).start())
        loop(gx + 1, 4, lambda x: to_x(g, x_ss.at[x], x).start())

        def step(z):
            b = 4 * z + gx
            arrived(kvx.at[b], blk_rs.at[b])
            for i in range(1, 4):
                to_x(b, fw_ss.at[z, i - 1], (gx + i) % 4).start()
        loop(0, zh, step)

    for h in range(HEADS):
        spread[h] = onehot(iota((128, TOK), 1) - 8 * (iota((128, TOK), 0) % 64) == off_ref[0, h])

    @pl.when(is_near)
    def _():
        inner = iota((256, 256), 0) // 64 < iota((256, 256), 1) // 64 + core
        for t in range(4):
            arrived(n_in.at[pl.ds(4 * t, 4)], n_rs.at[t])
            arrived(o_in.at[pl.ds(4 * t, 4)], o_rs.at[t])

            def part(b, side):
                x = n_in[4 * b:4 * b + 4, 0:64, :] if side == 0 else o_in[4 * b:4 * b + 4]
                return x.reshape(256, 128)

            for side in range(2):
                x = nt(eye, part(t, side))
                kvt[2 * t + side] = jnp.where(row_one, 1.0, x).astype(BF16)
            asks = []
            for i in range(4 * t, 4 * t + 4):
                x = n_in[i, 64:96, :].astype(F32)
                asks += [jnp.where(low, x, 0.0), jnp.where(low, turn(x), 0.0)]
            qt = jnp.concatenate(asks, axis=0).astype(BF16)
            m = None
            for n in range(2 * t + 2):
                x = nt(part(n // 2, n % 2), qt)
                if n // 2 == t:
                    x = jnp.where(causal if n % 2 == 0 else inner, x, NEG)
                scr[n] = x
                y = jnp.max(x, axis=0, keepdims=True)
                m = y if m is None else jnp.maximum(m, y)
            o = None
            for n in range(2 * t + 2):
                w = jnp.exp2((scr[n] - m) * C).astype(BF16)
                y = nn(kvt[n], w)
                o = y if o is None else o + y
            total = o[0:1]
            norm = o[64:128] / total
            lses = three(m * C + jnp.log(total) * math.log2(math.e))
            for jj in range(4):
                j = 4 * t + jj
                cols = slice(128 * (jj // 2), 128 * (jj // 2) + 128)
                top_half, bottom = norm[0:32, cols], norm[32:64, cols]
                ls = [x[:, cols] for x in lses]
                if jj % 2 == 0:
                    packed = jnp.where(low, top_half, turn(bottom))
                else:
                    packed = jnp.where(low, turn(top_half), bottom)
                tail = jnp.where(row16 == 0, ls[0], jnp.where(row16 == 1, ls[1], jnp.where(row16 == 2, ls[2], 0.0)))
                if jj % 2 == 1:
                    tail = turn(tail)
                ret_send[j, 0:32, :] = packed.astype(BF16)
                ret_send[j, 32:48, :] = tail.astype(BF16)
                send(ret_send.at[j], ret_in.at[head], ret_ss.at[0], ret_rs.at[head], 2 * j + core)

    @pl.when(is_far)
    def _():
        def step(b):
            @pl.when(b % 4 != gx)
            def _():
                arrived(kvx.at[b], blk_rs.at[b])
        loop(0, g, step)
        qf = qz[...]
        limit = iota((TOK, 128), 1) + 128 * g
        row = iota((TOK, 128), 0)

        def part(b):
            return kvx[4 * b:4 * b + 4].reshape(TOK, 128)

        m = None
        xs = []
        for b in range(4):
            x = nt(part(b), qf)
            x = jnp.where(row + TOK * b <= limit, x, NEG)
            xs.append(x)
            y = jnp.max(x, axis=0, keepdims=True)
            m = y if m is None else jnp.maximum(m, y)
        o = None
        for b in range(4):
            xt = nt(eye, part(b))
            xt = jnp.where(row_v, 1.0, xt).astype(BF16)
            y = nn(xt, jnp.exp2((xs[b] - m) * C).astype(BF16))
            o = y if o is None else o + y
        total = o[0:1]
        norm = (o[64:128] / total).astype(BF16)
        ls = three(m * C + jnp.log(total) * math.log2(math.e))
        r = iota((64, 128), 0)
        tail = jnp.where(r == 0, ls[0], jnp.where(r == 1, ls[1], jnp.where(r == 2, ls[2], 0.0)))
        both = jnp.concatenate([norm, tail.astype(BF16)], axis=0)
        i, j = iota((TOK, 128), 0), iota((TOK, 128), 1)
        place = onehot((j == 4 * (i // 16) + i % 16) & (i % 16 < 4))
        fret_send[...] = nt(place, both).astype(BF16).reshape(SEQ, 16, 128)
        loop(0, SEQ, lambda i: send(fret_send.at[i], fret_in.at[head], ret_ss.at[1], fret_rs.at[head], i))

    tok = iota((1, TOK), 1)
    low48 = iota((48, 128), 1) < HD
    zero = jnp.zeros((), BF16)
    for h in range(HEADS):
        arrived(ret_in.at[h], ret_rs.at[h])
        x = ret_in[h]
        left = jnp.concatenate([jnp.where(low48, x, zero), jnp.where(low, zero, x[0:32])], axis=0)
        u = nn(left, spread[h])
        l1 = jnp.where(tok % 8 == off_ref[0, h], u[32:33] + u[33:34] + u[34:35], NEG)
        arrived(fret_in.at[h], fret_rs.at[h])
        w = tn(fret_in[h], far_hot[h])
        l2 = jnp.where(tok % 128 == off_ref[1, h], w[64:65] + w[65:66] + w[66:67], NEG)
        m0 = top[h]
        big = jnp.maximum(jnp.maximum(m0, l1), l2)
        w0, w1, w2 = jnp.exp2(m0 - big), jnp.exp2(l1 - big), jnp.exp2(l2 - big)
        inv = 1.0 / (w0 * tot[h] + w1 + w2)
        w0, w1, w2 = w0 * inv, w1 * inv, w2 * inv
        for a in range(2):
            rows = slice(64 * h + 32 * a, 64 * h + 32 * a + 32)
            n1 = u[48 * a:48 * a + 32]
            n2 = w[32 * a:32 * a + 32]
            out_ref[rows, :] = (acc[rows, :] * w0 + n1 * w1 + n2 * w2).astype(BF16)

    sent(n_send.at[:, pl.ds(0, 64)], out_ss.at[2])

    @pl.when(is_near)
    def _():
        sent(n_send.at[pl.ds(0, HEADS - 1)], out_ss.at[1])
        sent(ret_send.at[pl.ds(0, 15)], ret_ss.at[0])

    @pl.when(jnp.logical_not(is_near))
    def _():
        sent(n_send, out_ss.at[1])

    @pl.when(is_far)
    def _():
        sent(f_send.at[pl.ds(0, HEADS - 1)], out_ss.at[0])
        sent(fret_send.at[pl.ds(0, SEQ - 1)], ret_ss.at[1])
        loop(gx + 1, 4, lambda x: to_x(g, x_ss.at[x], x).wait_send())
        loop(zh + 1, 4, lambda z: to_z(z).wait_send())

        def step(z):
            for i in range(1, 4):
                to_x(4 * z + gx, fw_ss.at[z, i - 1], (gx + i) % 4).wait_send()
        loop(0, zh, step)

    @pl.when(jnp.logical_not(is_far))
    def _():
        sent(f_send, out_ss.at[0])


def on_device(queries, keys, values, offsets, out_weight):
    hbm = pl.BlockSpec(memory_space=pltpu.HBM)
    vm = pltpu.VMEM
    dma = pltpu.SemaphoreType.DMA
    merged = pl.pallas_call(
        kernel,
        out_shape=jax.ShapeDtypeStruct((HEADS * HD, TOK), BF16),
        in_specs=[hbm, hbm, hbm, hbm],
        out_specs=pl.BlockSpec(memory_space=pltpu.VMEM),
        scratch_shapes=[
            vm((TOK, HEADS * HD), BF16),
            vm((TOK, HEADS * HD), BF16),
            vm((TOK, HEADS * HD), BF16),
            pltpu.SMEM((2, HEADS), jnp.int32),
            vm((HEADS, 96, 128), BF16),
            vm((HEADS, 16, 128), BF16),
            vm((16, 96, 128), BF16),
            vm((16, 64, 128), BF16),
            vm((SEQ, 16, 128), BF16),
            vm((128, 128), BF16),
            vm((8, 128, 256), BF16),
            vm((8, 256, 256), F32),
            vm((16, 48, 128), BF16),
            vm((HEADS, 48, 128), BF16),
            vm((GRP, 128, 128), BF16),
            vm((SEQ, 16, 128), BF16),
            vm((HEADS, 16, 128), BF16),
            vm((HEADS * HD, TOK), F32),
            vm((HEADS, 1, TOK), F32),
            vm((HEADS, 1, TOK), F32),
            vm((HEADS, 128, TOK), BF16),
            vm((HEADS, 16, TOK), BF16),
            dma((4,)), dma((3,)), dma((4,)), dma((4,)), dma,
            dma((4,)), dma((4,)), dma((3, 3)), dma((GRP,)),
            pltpu.SemaphoreType.REGULAR,
            dma((2,)), dma((HEADS,)), dma((HEADS,)),
        ],
        compiler_params=pltpu.CompilerParams(
            collective_id=0, has_side_effects=True, vmem_limit_bytes=56 * 1024 * 1024
        ),
    )(queries, keys, values, offsets)
    return tn(merged, out_weight).astype(BF16)


def solution(mesh):
    placed = (P(("grp", "seq"), None), P(("grp", "seq"), None), P(("grp", "seq"), None), P(), P())
    return jax.shard_map(
        on_device, mesh=mesh, in_specs=placed, out_specs=P(("grp", "seq"), None), check_vma=False
    )
```

```python
import math

import jax
import jax.numpy as jnp
from jax import lax
from jax.experimental import pallas as pl
from jax.experimental.pallas import tpu as pltpu
from jax.sharding import PartitionSpec as P

MESH = pl.DeviceIdType.MESH
HEADS = 6
HD = 64
TOK = 512
SEQ = 32
GRP = 16
NEG = -1e30
C = math.log2(math.e) / math.sqrt(HD)
F32 = jnp.float32
BF16 = jnp.bfloat16


def nt(a, b):
    return lax.dot_general(a, b, (((1,), (1,)), ((), ())), preferred_element_type=F32)


def nn(a, b):
    return lax.dot_general(a, b, (((1,), (0,)), ((), ())), preferred_element_type=F32)


def tn(a, b):
    return lax.dot_general(a, b, (((0,), (0,)), ((), ())), preferred_element_type=F32)


def iota(shape, dim):
    return lax.broadcasted_iota(jnp.int32, shape, dim)


def onehot(cond):
    return jnp.where(cond, 1.0, 0.0).astype(BF16)


def near_chip(h):
    return (5 * h + 1) % 16


def far_chip(h):
    return (5 * (h + 6) + 1) % 16


def turn(x):
    return pltpu.roll(x, HD, 1)


def three(x):
    hi = x.astype(BF16).astype(F32)
    rest = x - hi
    mid = rest.astype(BF16).astype(F32)
    return hi, mid, rest - mid


def loop(lo, hi, f):
    def step(i, c):
        f(i)
        return c

    lax.fori_loop(lo, hi, step, 0)


def kernel(
    q_hbm, k_hbm, v_hbm, off_hbm, out_ref,
    q_ref, k_ref, v_ref, off_ref,
    n_send, f_send, n_in, o_in, f_in, g_in, qz, kvt, scr, ret_send, ret_in,
    kvx, fret_send, fret_in, acc, top, tot, spread, far_hot, far_m, far_o,
    in_sem, out_ss, n_rs, o_rs, f_rs, g_rs, z_ss, x_ss, blk_rs, go, ret_ss, ret_rs, fret_rs,
):
    s = lax.axis_index("seq")
    g = lax.axis_index("grp")
    chip, core = s // 2, s % 2
    zh, gx = g // 4, g % 4
    role = ((chip + 15) * 13) % 16
    is_near = role < HEADS
    on_far = (role >= HEADS) & (role < 2 * HEADS)
    is_far = on_far & (core == 0)
    head = role % HEADS
    sibling = s + 1 - 2 * core

    inputs = [
        pltpu.make_async_copy(src, dst, in_sem.at[i])
        for i, (src, dst) in enumerate(
            ((off_hbm, off_ref), (q_hbm, q_ref), (k_hbm, k_ref), (v_hbm, v_ref))
        )
    ]
    for c in inputs:
        c.start()

    barrier = pltpu.get_barrier_semaphore()

    def far_seat(i):
        part = ((i // 2 + 15) * 13) % 16
        return (part >= HEADS) & (part < 2 * HEADS) & (i % 2 == 0) & (zh < 2)

    def hello(axis, target):
        pl.semaphore_signal(barrier, inc=1, device_id={axis: target}, device_id_type=MESH)

    @pl.when(is_near | is_far)
    def _():
        def step(i):
            @pl.when((i != s) & jnp.logical_not(far_seat(i)))
            def _():
                hello("seq", i)
        loop(0, SEQ, step)

    @pl.when(is_far)
    def _():
        for i in range(1, 4):
            pl.semaphore_signal(
                barrier, inc=1, device_id={"grp": 4 * zh + (gx + i) % 4, "seq": sibling}, device_id_type=MESH
            )

        @pl.when((zh == 1) | (zh == 2))
        def _():
            hello("grp", g - 4)

        @pl.when(zh == 3)
        def _():
            hello("grp", g - 12)
            hello("grp", g - 8)

            loop(0, SEQ, lambda i: pl.semaphore_signal(
                barrier, inc=1, device_id={"grp": g - 4, "seq": i}, device_id_type=MESH
            ))

    low = iota((32, 128), 1) < HD
    low16 = iota((16, 128), 1) < HD
    row16 = iota((16, 128), 0)
    near_diff = iota((32, 256), 1) - 8 * iota((32, 256), 0)
    fr = iota((16, TOK), 0)
    far_diff = jnp.where(fr < 8, iota((16, TOK), 1) - 128 * (fr % 4), -1)
    for c in inputs:
        c.wait()
    for p in range(3):
        near_hot = [onehot(near_diff == off_ref[0, 2 * p + e]) for e in range(2)]
        hot = [onehot(far_diff == off_ref[1, 2 * p + e]) for e in range(2)]
        for e in range(2):
            far_hot[2 * p + e] = hot[e]
        picked = []
        for ref in (q_ref, k_ref, v_ref):
            halves = []
            for a in range(2):
                left = jnp.concatenate(near_hot + [f[:, 256 * a:256 * a + 256] for f in hot], axis=0)
                halves.append(nn(left, ref[256 * a:256 * a + 256, 128 * p:128 * p + 128]))
            picked.append(halves)
        pq, pk, pv = picked
        for e in range(2):
            h = 2 * p + e
            for a in range(2):
                rk, rv = pk[a][32 * e:32 * e + 32], pv[a][32 * e:32 * e + 32]
                kv = jnp.where(low, rk, turn(rv)) if e == 0 else jnp.where(low, turn(rk), rv)
                n_send[h, 32 * a:32 * a + 32, :] = kv.astype(BF16)
            r0, r1 = pq[0][32 * e:32 * e + 32], pq[1][32 * e:32 * e + 32]
            qq = jnp.where(low, r0, turn(r1)) if e == 0 else jnp.where(low, turn(r0), r1)
            n_send[h, 64:96, :] = qq.astype(BF16)
            lo = 64 + 16 * e
            fq, fk, fv = [x[0][lo:lo + 16] + x[1][lo:lo + 16] for x in (pq, pk, pv)]
            if e == 0:
                fkv, fqz = jnp.where(low16, fk, turn(fv)), fq
            else:
                fkv, fqz = jnp.where(low16, turn(fk), fv), turn(fq)
            tile = jnp.where(row16 < 4, fkv, jnp.where(low16 & (row16 < 8), fqz, 0.0))
            f_send[h] = tile.astype(BF16)

    ahead = jnp.where(zh == 2, HEADS, 0)

    @pl.when(is_near | (is_far & (zh > 1)))
    def _():
        pl.semaphore_wait(barrier, 3 * HEADS - 1 + ahead)

    @pl.when(jnp.logical_not(is_near | on_far))
    def _():
        pl.semaphore_wait(barrier, 3 * HEADS + ahead)

    @pl.when(on_far & (core == 1))
    def _():
        pl.semaphore_wait(barrier, 3 * HEADS + 3 + ahead)
        pl.semaphore_signal(go, inc=1, device_id={"seq": sibling}, device_id_type=MESH)

    @pl.when(is_far & (zh < 2))
    def _():
        pl.semaphore_wait(go, 1)

    def copy(src, dst, ss, rs, target, axis="seq"):
        return pltpu.make_async_remote_copy(
            src_ref=src, dst_ref=dst, send_sem=ss, recv_sem=rs, device_id={axis: target}, device_id_type=MESH
        )

    def send(src, dst, ss, rs, target):
        @pl.when(s == target)
        def _():
            pltpu.make_async_copy(src, dst, rs).start()

        @pl.when(s != target)
        def _():
            copy(src, dst, ss, rs, target).start()

    def arrived(dst, rs):
        copy(dst, dst, in_sem.at[0], rs, sibling).wait_recv()

    def sent(src, ss):
        copy(src, src, ss, in_sem.at[0], sibling).wait_send()

    for i in range(HEADS):
        h = (chip + i) % HEADS
        send(f_send.at[h], f_in.at[s], out_ss.at[0], f_rs, 2 * far_chip(h))
    def early(h):
        return pltpu.make_async_remote_copy(
            src_ref=f_send.at[h], dst_ref=g_in.at[s], send_sem=out_ss.at[3], recv_sem=g_rs,
            device_id={"grp": g + 4, "seq": 2 * far_chip(h)}, device_id_type=MESH,
        )

    @pl.when(zh == 2)
    def _():
        for i in range(HEADS):
            early((chip + i) % HEADS).start()

    for i in range(HEADS):
        h = (chip + i) % HEADS
        send(n_send.at[h], n_in.at[chip], out_ss.at[1], n_rs.at[chip // 4], 2 * near_chip(h) + core)
    for i in range(HEADS):
        h = (chip + i) % HEADS
        copy(
            n_send.at[h, pl.ds(0, 64)], o_in.at[chip], out_ss.at[2], o_rs.at[chip // 4], 2 * near_chip(h) + 1 - core
        ).start()

    eye = onehot(iota((128, 128), 0) == iota((128, 128), 1))
    causal = iota((256, 256), 0) <= iota((256, 256), 1)
    lane_q = iota((TOK, 128), 1) < HD
    row_v = iota((128, TOK), 0) < HD
    row_one = iota((128, 256), 0) < HD

    def local_pair(p):
        cols = slice(128 * p, 128 * p + 128)
        kp, qp, vp = k_ref[:, cols], q_ref[:, cols], v_ref[:, cols]
        vt = nt(eye, vp)
        for e in range(2):
            h = 2 * p + e
            mine = lane_q if e == 0 else jnp.logical_not(lane_q)
            qe = jnp.where(mine, qp, jnp.zeros((), BF16))
            mine_v = row_v if e == 0 else jnp.logical_not(row_v)
            ve = jnp.where(mine_v, vt, 1.0).astype(BF16)
            for t in range(2):
                qt = qe[256 * t:256 * t + 256]
                parts = [nt(kp[256 * b:256 * b + 256], qt) for b in range(t + 1)]
                parts[t] = jnp.where(causal, parts[t], NEG)
                m = jnp.max(parts[0], axis=0, keepdims=True)
                for x in parts[1:]:
                    m = jnp.maximum(m, jnp.max(x, axis=0, keepdims=True))
                o = None
                for b, x in enumerate(parts):
                    w = jnp.exp2((x - m) * C).astype(BF16)
                    y = nn(ve[:, 256 * b:256 * b + 256], w)
                    o = y if o is None else o + y
                ts = slice(256 * t, 256 * t + 256)
                acc[64 * h:64 * h + 64, ts] = o[64 * e:64 * e + 64]
                other = 64 * (1 - e)
                tot[h, :, ts] = o[other:other + 1]
                top[h, :, ts] = m * C

    def to_group(b, ss, i):
        return copy(kvx.at[b], kvx.at[b], ss, blk_rs.at[b], i, "grp")

    def on_z(i):
        return to_group(g, z_ss.at[i], jnp.where((zh == 0) & (i == 1), g + 12, g + 4 + 4 * i))

    def on_z_pass():
        return to_group(gx, z_ss.at[2], g + 4)

    def on_x(b, i):
        return to_group(b, x_ss.at[b // 4, i - 1], 4 * zh + (gx + i) % 4)

    for p in range(3):
        local_pair(p)

    @pl.when(is_far)
    def _():
        def clear(b):
            kvx[b] = jnp.zeros((128, 128), BF16)
        loop(g + 1, 4 * zh + 4, clear)
        arrived(f_in, f_rs)
        i, j = iota((128, TOK), 0), iota((128, TOK), 1)
        base = 16 * (i // 4) + i % 4
        keys = onehot(j == base)
        rows = f_in[...].reshape(TOK, 128)
        kvx[g] = nn(keys, rows).astype(BF16)
        qz[...] = nn(onehot(j == base + 4), rows).astype(BF16)

        @pl.when(zh > 1)
        def _():
            pl.semaphore_wait(go, 1)
        for i in range(1, 4):
            @pl.when(gx + i < 4)
            def _():
                on_x(g, i).start()

        @pl.when(zh < 2)
        def _():
            pl.semaphore_wait(barrier, 2)
            for i in range(2):
                on_z(i).start()

        @pl.when(zh == 3)
        def _():
            arrived(g_in, g_rs)
            kvx[g - 4] = nn(keys, g_in[...].reshape(TOK, 128)).astype(BF16)
            for i in range(1, 4):
                on_x(g - 4, i).start()

        def passing(z):
            b = 4 * z + gx
            arrived(kvx.at[b], blk_rs.at[b])

            @pl.when(zh == 1)
            def _():
                on_z_pass().start()
            for i in range(1, 4):
                on_x(b, i).start()
        loop(0, jnp.minimum(zh, 2), passing)

    for h in range(HEADS):
        spread[h] = onehot(iota((128, TOK), 1) - 8 * (iota((128, TOK), 0) % 64) == off_ref[0, h])

    @pl.when(is_near)
    def _():
        inner = iota((256, 256), 0) // 64 < iota((256, 256), 1) // 64 + core
        for t in range(4):
            arrived(n_in.at[pl.ds(4 * t, 4)], n_rs.at[t])
            arrived(o_in.at[pl.ds(4 * t, 4)], o_rs.at[t])

            def part(b, side):
                x = n_in[4 * b:4 * b + 4, 0:64, :] if side == 0 else o_in[4 * b:4 * b + 4]
                return x.reshape(256, 128)

            for side in range(2):
                x = nt(eye, part(t, side))
                kvt[2 * t + side] = jnp.where(row_one, 1.0, x).astype(BF16)
            asks = []
            for i in range(4 * t, 4 * t + 4):
                x = n_in[i, 64:96, :].astype(F32)
                asks += [jnp.where(low, x, 0.0), jnp.where(low, turn(x), 0.0)]
            qt = jnp.concatenate(asks, axis=0).astype(BF16)
            m = None
            for n in range(2 * t + 2):
                x = nt(part(n // 2, n % 2), qt)
                if n // 2 == t:
                    x = jnp.where(causal if n % 2 == 0 else inner, x, NEG)
                scr[n] = x
                y = jnp.max(x, axis=0, keepdims=True)
                m = y if m is None else jnp.maximum(m, y)
            o = None
            for n in range(2 * t + 2):
                w = jnp.exp2((scr[n] - m) * C).astype(BF16)
                y = nn(kvt[n], w)
                o = y if o is None else o + y
            total = o[0:1]
            norm = o[64:128] / total
            lses = three(m * C + jnp.log(total) * math.log2(math.e))
            for jj in range(4):
                j = 4 * t + jj
                cols = slice(128 * (jj // 2), 128 * (jj // 2) + 128)
                top_half, bottom = norm[0:32, cols], norm[32:64, cols]
                ls = [x[:, cols] for x in lses]
                if jj % 2 == 0:
                    packed = jnp.where(low, top_half, turn(bottom))
                else:
                    packed = jnp.where(low, turn(top_half), bottom)
                tail = jnp.where(row16 == 0, ls[0], jnp.where(row16 == 1, ls[1], jnp.where(row16 == 2, ls[2], 0.0)))
                if jj % 2 == 1:
                    tail = turn(tail)
                ret_send[j, 0:32, :] = packed.astype(BF16)
                ret_send[j, 32:48, :] = tail.astype(BF16)
                send(ret_send.at[j], ret_in.at[head], ret_ss.at[0], ret_rs.at[head], 2 * j + core)

    @pl.when(is_far)
    def _():
        qf = qz[...]
        limit = iota((TOK, 128), 1) - iota((TOK, 128), 0)
        far_m[...] = jnp.full((1, 128), NEG, F32)
        far_o[...] = jnp.zeros((128, 128), F32)

        def slab(n):
            z = jnp.where((zh == 3) & (n > 1), 5 - n, n)

            def wait(b):
                @pl.when(b % 4 != gx)
                def _():
                    arrived(kvx.at[b], blk_rs.at[b])
            loop(4 * z, jnp.minimum(4 * z + 4, g), wait)
            part = kvx[pl.ds(4 * z, 4)].reshape(TOK, 128)
            x = jnp.where(limit >= TOK * z - 128 * g, nt(part, qf), NEG)
            old = far_m[...]
            new = jnp.maximum(old, jnp.max(x, axis=0, keepdims=True))
            xt = jnp.where(row_v, 1.0, nt(eye, part)).astype(BF16)
            y = nn(xt, jnp.exp2((x - new) * C).astype(BF16))
            far_o[...] = far_o[...] * jnp.exp2((old - new) * C) + y
            far_m[...] = new
        loop(0, zh + 1, slab)
        m, o = far_m[...], far_o[...]
        total = o[0:1]
        norm = (o[64:128] / total).astype(BF16)
        ls = three(m * C + jnp.log(total) * math.log2(math.e))
        r = iota((64, 128), 0)
        tail = jnp.where(r == 0, ls[0], jnp.where(r == 1, ls[1], jnp.where(r == 2, ls[2], 0.0)))
        both = jnp.concatenate([norm, tail.astype(BF16)], axis=0)
        i, j = iota((TOK, 128), 0), iota((TOK, 128), 1)
        place = onehot((j == 4 * (i // 16) + i % 16) & (i % 16 < 4))
        fret_send[...] = nt(place, both).astype(BF16).reshape(SEQ, 16, 128)
        loop(0, SEQ, lambda i: send(fret_send.at[i], fret_in.at[head], ret_ss.at[1], fret_rs.at[head], i))

    tok = iota((1, TOK), 1)
    low48 = iota((48, 128), 1) < HD
    zero = jnp.zeros((), BF16)
    for h in range(HEADS):
        arrived(ret_in.at[h], ret_rs.at[h])
        x = ret_in[h]
        left = jnp.concatenate([jnp.where(low48, x, zero), jnp.where(low, zero, x[0:32])], axis=0)
        u = nn(left, spread[h])
        l1 = jnp.where(tok % 8 == off_ref[0, h], u[32:33] + u[33:34] + u[34:35], NEG)
        m0 = top[h]
        big = jnp.maximum(m0, l1)
        w0, w1 = jnp.exp2(m0 - big), jnp.exp2(l1 - big)
        top[h] = big
        tot[h] = w0 * tot[h] + w1
        for a in range(2):
            rows = slice(64 * h + 32 * a, 64 * h + 32 * a + 32)
            acc[rows, :] = acc[rows, :] * w0 + u[48 * a:48 * a + 32] * w1
    for h in range(HEADS):
        arrived(fret_in.at[h], fret_rs.at[h])
        w = tn(fret_in[h], far_hot[h])
        l2 = jnp.where(tok % 128 == off_ref[1, h], w[64:65] + w[65:66] + w[66:67], NEG)
        m0 = top[h]
        big = jnp.maximum(m0, l2)
        w0, w2 = jnp.exp2(m0 - big), jnp.exp2(l2 - big)
        inv = 1.0 / (w0 * tot[h] + w2)
        rows = slice(64 * h, 64 * h + 64)
        out_ref[rows, :] = (acc[rows, :] * (w0 * inv) + w[0:64] * (w2 * inv)).astype(BF16)

    sent(n_send.at[:, pl.ds(0, 64)], out_ss.at[2])

    @pl.when(zh == 2)
    def _():
        sent(f_send, out_ss.at[3])

    @pl.when(is_near)
    def _():
        sent(n_send.at[pl.ds(0, HEADS - 1)], out_ss.at[1])
        sent(ret_send.at[pl.ds(0, 15)], ret_ss.at[0])

    @pl.when(jnp.logical_not(is_near))
    def _():
        sent(n_send, out_ss.at[1])

    @pl.when(is_far)
    def _():
        sent(f_send.at[pl.ds(0, HEADS - 1)], out_ss.at[0])
        sent(fret_send.at[pl.ds(0, SEQ - 1)], ret_ss.at[1])
        for i in range(1, 4):
            @pl.when(gx + i < 4)
            def _():
                on_x(g, i).wait_send()

            loop(0, zh, lambda z: on_x(4 * z + gx, i).wait_send())

        @pl.when(zh < 2)
        def _():
            for i in range(2):
                on_z(i).wait_send()

        @pl.when(zh == 1)
        def _():
            on_z_pass().wait_send()

    @pl.when(jnp.logical_not(is_far))
    def _():
        sent(f_send, out_ss.at[0])


def on_device(queries, keys, values, offsets, out_weight):
    hbm = pl.BlockSpec(memory_space=pltpu.HBM)
    vm = pltpu.VMEM
    dma = pltpu.SemaphoreType.DMA
    merged = pl.pallas_call(
        kernel,
        out_shape=jax.ShapeDtypeStruct((HEADS * HD, TOK), BF16),
        in_specs=[hbm, hbm, hbm, hbm],
        out_specs=pl.BlockSpec(memory_space=pltpu.VMEM),
        scratch_shapes=[
            vm((TOK, HEADS * HD), BF16),
            vm((TOK, HEADS * HD), BF16),
            vm((TOK, HEADS * HD), BF16),
            pltpu.SMEM((2, HEADS), jnp.int32),
            vm((HEADS, 96, 128), BF16),
            vm((HEADS, 16, 128), BF16),
            vm((16, 96, 128), BF16),
            vm((16, 64, 128), BF16),
            vm((SEQ, 16, 128), BF16),
            vm((SEQ, 16, 128), BF16),
            vm((128, 128), BF16),
            vm((8, 128, 256), BF16),
            vm((8, 256, 256), F32),
            vm((16, 48, 128), BF16),
            vm((HEADS, 48, 128), BF16),
            vm((GRP, 128, 128), BF16),
            vm((SEQ, 16, 128), BF16),
            vm((HEADS, 16, 128), BF16),
            vm((HEADS * HD, TOK), F32),
            vm((HEADS, 1, TOK), F32),
            vm((HEADS, 1, TOK), F32),
            vm((HEADS, 128, TOK), BF16),
            vm((HEADS, 16, TOK), BF16),
            vm((1, 128), F32),
            vm((128, 128), F32),
            dma((4,)), dma((4,)), dma((4,)), dma((4,)), dma, dma,
            dma((3,)), dma((4, 3)), dma((GRP,)),
            pltpu.SemaphoreType.REGULAR,
            dma((2,)), dma((HEADS,)), dma((HEADS,)),
        ],
        compiler_params=pltpu.CompilerParams(
            collective_id=0, has_side_effects=True, vmem_limit_bytes=55783424
        ),
    )(queries, keys, values, offsets)
    return tn(merged, out_weight).astype(BF16)


def solution(mesh):
    placed = (P(("grp", "seq"), None), P(("grp", "seq"), None), P(("grp", "seq"), None), P(), P())
    return jax.shard_map(
        on_device, mesh=mesh, in_specs=placed, out_specs=P(("grp", "seq"), None), check_vma=False
    )
```

```python
import math

import jax
import jax.numpy as jnp
from jax import lax
from jax.experimental import pallas as pl
from jax.experimental.pallas import tpu as pltpu
from jax.sharding import PartitionSpec as P

MESH = pl.DeviceIdType.MESH
HEADS = 6
HD = 64
TOK = 512
SEQ = 32
GRP = 16
NEG = -1e30
C = math.log2(math.e) / math.sqrt(HD)
F32 = jnp.float32
BF16 = jnp.bfloat16


def nt(a, b):
    return lax.dot_general(a, b, (((1,), (1,)), ((), ())), preferred_element_type=F32)


def nn(a, b):
    return lax.dot_general(a, b, (((1,), (0,)), ((), ())), preferred_element_type=F32)


def tn(a, b):
    return lax.dot_general(a, b, (((0,), (0,)), ((), ())), preferred_element_type=F32)


def iota(shape, dim):
    return lax.broadcasted_iota(jnp.int32, shape, dim)


def onehot(cond):
    return jnp.where(cond, 1.0, 0.0).astype(BF16)


def near_chip(h):
    return (5 * h + 1) % 16


def far_chip(h):
    return (5 * (h + 6) + 1) % 16


def turn(x):
    return pltpu.roll(x, HD, 1)


def three(x):
    hi = x.astype(BF16).astype(F32)
    rest = x - hi
    mid = rest.astype(BF16).astype(F32)
    return hi, mid, rest - mid


def loop(lo, hi, f):
    def step(i, c):
        f(i)
        return c

    lax.fori_loop(lo, hi, step, 0)


def kernel(
    q_hbm, k_hbm, v_hbm, off_hbm, out_ref,
    q_ref, k_ref, v_ref, off_ref,
    n_send, f_send, n_in, o_in, f_in, g_in, qz, kvt, scr, ret_send, ret_in,
    kvx, fret_send, fret_in, acc, top, tot, spread, far_hot, far_m, far_o,
    in_sem, out_ss, n_rs, o_rs, f_rs, g_rs, z_ss, x_ss, blk_rs, go, ret_ss, ret_rs, fret_rs,
):
    s = lax.axis_index("seq")
    g = lax.axis_index("grp")
    chip, core = s // 2, s % 2
    zh, gx = g // 4, g % 4
    role = ((chip + 15) * 13) % 16
    is_near = role < HEADS
    on_far = (role >= HEADS) & (role < 2 * HEADS)
    is_far = on_far & (core == 0)
    head = role % HEADS
    sibling = s + 1 - 2 * core

    inputs = [
        pltpu.make_async_copy(src, dst, in_sem.at[i])
        for i, (src, dst) in enumerate(
            ((off_hbm, off_ref), (q_hbm, q_ref), (k_hbm, k_ref), (v_hbm, v_ref))
        )
    ]
    for c in inputs:
        c.start()

    barrier = pltpu.get_barrier_semaphore()

    def far_seat(i):
        part = ((i // 2 + 15) * 13) % 16
        return (part >= HEADS) & (part < 2 * HEADS) & (i % 2 == 0) & (zh < 2)

    def hello(axis, target):
        pl.semaphore_signal(barrier, inc=1, device_id={axis: target}, device_id_type=MESH)

    @pl.when(is_far)
    def _():
        for i in range(1, 4):
            pl.semaphore_signal(
                barrier, inc=1, device_id={"grp": 4 * zh + (gx + i) % 4, "seq": sibling}, device_id_type=MESH
            )

        @pl.when((zh == 1) | (zh == 2))
        def _():
            hello("grp", g - 4)

        @pl.when(zh == 3)
        def _():
            hello("grp", g - 12)
            hello("grp", g - 8)

            loop(0, SEQ, lambda i: pl.semaphore_signal(
                barrier, inc=1, device_id={"grp": g - 4, "seq": i}, device_id_type=MESH
            ))

    @pl.when(is_near | is_far)
    def _():
        def step(i):
            @pl.when((i != s) & jnp.logical_not(far_seat(i)))
            def _():
                hello("seq", i)
        loop(0, SEQ, step)

    low = iota((32, 128), 1) < HD
    low16 = iota((16, 128), 1) < HD
    row16 = iota((16, 128), 0)
    near_diff = iota((32, 256), 1) - 8 * iota((32, 256), 0)
    fr = iota((16, TOK), 0)
    far_diff = jnp.where(fr < 8, iota((16, TOK), 1) - 128 * (fr % 4), -1)
    for c in inputs:
        c.wait()
    for p in range(3):
        near_hot = [onehot(near_diff == off_ref[0, 2 * p + e]) for e in range(2)]
        hot = [onehot(far_diff == off_ref[1, 2 * p + e]) for e in range(2)]
        for e in range(2):
            far_hot[2 * p + e] = hot[e]
        picked = []
        for ref in (q_ref, k_ref, v_ref):
            halves = []
            for a in range(2):
                left = jnp.concatenate(near_hot + [f[:, 256 * a:256 * a + 256] for f in hot], axis=0)
                halves.append(nn(left, ref[256 * a:256 * a + 256, 128 * p:128 * p + 128]))
            picked.append(halves)
        pq, pk, pv = picked
        for e in range(2):
            h = 2 * p + e
            for a in range(2):
                rk, rv = pk[a][32 * e:32 * e + 32], pv[a][32 * e:32 * e + 32]
                kv = jnp.where(low, rk, turn(rv)) if e == 0 else jnp.where(low, turn(rk), rv)
                n_send[h, 32 * a:32 * a + 32, :] = kv.astype(BF16)
            r0, r1 = pq[0][32 * e:32 * e + 32], pq[1][32 * e:32 * e + 32]
            qq = jnp.where(low, r0, turn(r1)) if e == 0 else jnp.where(low, turn(r0), r1)
            n_send[h, 64:96, :] = qq.astype(BF16)
            lo = 64 + 16 * e
            fq, fk, fv = [x[0][lo:lo + 16] + x[1][lo:lo + 16] for x in (pq, pk, pv)]
            if e == 0:
                fkv, fqz = jnp.where(low16, fk, turn(fv)), fq
            else:
                fkv, fqz = jnp.where(low16, turn(fk), fv), turn(fq)
            tile = jnp.where(row16 < 4, fkv, jnp.where(low16 & (row16 < 8), fqz, 0.0))
            f_send[h] = tile.astype(BF16)

    ahead = jnp.where(zh == 2, HEADS, 0)

    @pl.when(is_near | (is_far & (zh > 1)))
    def _():
        pl.semaphore_wait(barrier, 3 * HEADS - 1 + ahead)

    @pl.when(jnp.logical_not(is_near | on_far))
    def _():
        pl.semaphore_wait(barrier, 3 * HEADS + ahead)

    @pl.when(on_far & (core == 1))
    def _():
        pl.semaphore_wait(barrier, 3 * HEADS + 3 + ahead)
        pl.semaphore_signal(go, inc=1, device_id={"seq": sibling}, device_id_type=MESH)

    @pl.when(is_far & (zh < 2))
    def _():
        pl.semaphore_wait(go, 1)

    def copy(src, dst, ss, rs, target, axis="seq"):
        return pltpu.make_async_remote_copy(
            src_ref=src, dst_ref=dst, send_sem=ss, recv_sem=rs, device_id={axis: target}, device_id_type=MESH
        )

    def send(src, dst, ss, rs, target):
        @pl.when(s == target)
        def _():
            pltpu.make_async_copy(src, dst, rs).start()

        @pl.when(s != target)
        def _():
            copy(src, dst, ss, rs, target).start()

    def arrived(dst, rs):
        copy(dst, dst, in_sem.at[0], rs, sibling).wait_recv()

    def sent(src, ss):
        copy(src, src, ss, in_sem.at[0], sibling).wait_send()

    for i in range(HEADS):
        h = (chip + i) % HEADS
        send(f_send.at[h], f_in.at[s], out_ss.at[0], f_rs, 2 * far_chip(h))
    def early(h):
        return pltpu.make_async_remote_copy(
            src_ref=f_send.at[h], dst_ref=g_in.at[s], send_sem=out_ss.at[3], recv_sem=g_rs,
            device_id={"grp": g + 4, "seq": 2 * far_chip(h)}, device_id_type=MESH,
        )

    @pl.when(zh == 2)
    def _():
        for i in range(HEADS):
            early((chip + i) % HEADS).start()

    for i in range(HEADS):
        h = (chip + i) % HEADS
        send(n_send.at[h], n_in.at[chip], out_ss.at[1], n_rs.at[chip // 4], 2 * near_chip(h) + core)
    for i in range(HEADS):
        h = (chip + i) % HEADS
        copy(
            n_send.at[h, pl.ds(0, 64)], o_in.at[chip], out_ss.at[2], o_rs.at[chip // 4], 2 * near_chip(h) + 1 - core
        ).start()

    eye = onehot(iota((128, 128), 0) == iota((128, 128), 1))
    causal = iota((256, 256), 0) <= iota((256, 256), 1)
    lane_q = iota((TOK, 128), 1) < HD
    row_v = iota((128, TOK), 0) < HD
    row_one = iota((128, 256), 0) < HD

    def local_pair(p):
        cols = slice(128 * p, 128 * p + 128)
        kp, qp, vp = k_ref[:, cols], q_ref[:, cols], v_ref[:, cols]
        vt = nt(eye, vp)
        for e in range(2):
            h = 2 * p + e
            mine = lane_q if e == 0 else jnp.logical_not(lane_q)
            qe = jnp.where(mine, qp, jnp.zeros((), BF16))
            mine_v = row_v if e == 0 else jnp.logical_not(row_v)
            ve = jnp.where(mine_v, vt, 1.0).astype(BF16)
            for t in range(2):
                qt = qe[256 * t:256 * t + 256]
                parts = [nt(kp[256 * b:256 * b + 256], qt) for b in range(t + 1)]
                parts[t] = jnp.where(causal, parts[t], NEG)
                m = jnp.max(parts[0], axis=0, keepdims=True)
                for x in parts[1:]:
                    m = jnp.maximum(m, jnp.max(x, axis=0, keepdims=True))
                o = None
                for b, x in enumerate(parts):
                    w = jnp.exp2((x - m) * C).astype(BF16)
                    y = nn(ve[:, 256 * b:256 * b + 256], w)
                    o = y if o is None else o + y
                ts = slice(256 * t, 256 * t + 256)
                acc[64 * h:64 * h + 64, ts] = o[64 * e:64 * e + 64]
                other = 64 * (1 - e)
                tot[h, :, ts] = o[other:other + 1]
                top[h, :, ts] = m * C

    def to_group(b, ss, i):
        return copy(kvx.at[b], kvx.at[b], ss, blk_rs.at[b], i, "grp")

    def on_z(i):
        return to_group(g, z_ss.at[i], jnp.where((zh == 0) & (i == 1), g + 12, g + 4 + 4 * i))

    def on_z_pass():
        return to_group(gx, z_ss.at[2], g + 4)

    def on_x(b, i):
        return to_group(b, x_ss.at[b // 4, i - 1], 4 * zh + (gx + i) % 4)

    for p in range(3):
        local_pair(p)

    @pl.when(is_far)
    def _():
        def clear(b):
            kvx[b] = jnp.zeros((128, 128), BF16)
        loop(g + 1, 4 * zh + 4, clear)
        arrived(f_in, f_rs)
        i, j = iota((128, TOK), 0), iota((128, TOK), 1)
        base = 16 * (i // 4) + i % 4
        keys = onehot(j == base)
        rows = f_in[...].reshape(TOK, 128)
        kvx[g] = nn(keys, rows).astype(BF16)
        qz[...] = nn(onehot(j == base + 4), rows).astype(BF16)

        @pl.when(zh > 1)
        def _():
            pl.semaphore_wait(go, 1)
        for i in range(1, 4):
            @pl.when(gx + i < 4)
            def _():
                on_x(g, i).start()

        @pl.when(zh < 2)
        def _():
            pl.semaphore_wait(barrier, 2)
            for i in range(2):
                on_z(i).start()

        @pl.when(zh == 3)
        def _():
            arrived(g_in, g_rs)
            kvx[g - 4] = nn(keys, g_in[...].reshape(TOK, 128)).astype(BF16)
            for i in range(1, 4):
                on_x(g - 4, i).start()

        def passing(z):
            b = 4 * z + gx
            arrived(kvx.at[b], blk_rs.at[b])

            @pl.when(zh == 1)
            def _():
                on_z_pass().start()
            for i in range(1, 4):
                on_x(b, i).start()
        loop(0, jnp.minimum(zh, 2), passing)

    for h in range(HEADS):
        spread[h] = onehot(iota((128, TOK), 1) - 8 * (iota((128, TOK), 0) % 64) == off_ref[0, h])

    @pl.when(is_near)
    def _():
        inner = iota((256, 256), 0) // 64 < iota((256, 256), 1) // 64 + core
        for t in range(4):
            arrived(n_in.at[pl.ds(4 * t, 4)], n_rs.at[t])
            arrived(o_in.at[pl.ds(4 * t, 4)], o_rs.at[t])

            def part(b, side):
                x = n_in[4 * b:4 * b + 4, 0:64, :] if side == 0 else o_in[4 * b:4 * b + 4]
                return x.reshape(256, 128)

            for side in range(2):
                x = nt(eye, part(t, side))
                kvt[2 * t + side] = jnp.where(row_one, 1.0, x).astype(BF16)
            asks = []
            for i in range(4 * t, 4 * t + 4):
                x = n_in[i, 64:96, :].astype(F32)
                asks += [jnp.where(low, x, 0.0), jnp.where(low, turn(x), 0.0)]
            qt = jnp.concatenate(asks, axis=0).astype(BF16)
            m = None
            for n in range(2 * t + 2):
                x = nt(part(n // 2, n % 2), qt)
                if n // 2 == t:
                    x = jnp.where(causal if n % 2 == 0 else inner, x, NEG)
                scr[n] = x
                y = jnp.max(x, axis=0, keepdims=True)
                m = y if m is None else jnp.maximum(m, y)
            o = None
            for n in range(2 * t + 2):
                w = jnp.exp2((scr[n] - m) * C).astype(BF16)
                y = nn(kvt[n], w)
                o = y if o is None else o + y
            total = o[0:1]
            norm = o[64:128] / total
            lses = three(m * C + jnp.log(total) * math.log2(math.e))
            for jj in range(4):
                j = 4 * t + jj
                cols = slice(128 * (jj // 2), 128 * (jj // 2) + 128)
                top_half, bottom = norm[0:32, cols], norm[32:64, cols]
                ls = [x[:, cols] for x in lses]
                if jj % 2 == 0:
                    packed = jnp.where(low, top_half, turn(bottom))
                else:
                    packed = jnp.where(low, turn(top_half), bottom)
                tail = jnp.where(row16 == 0, ls[0], jnp.where(row16 == 1, ls[1], jnp.where(row16 == 2, ls[2], 0.0)))
                if jj % 2 == 1:
                    tail = turn(tail)
                ret_send[j, 0:32, :] = packed.astype(BF16)
                ret_send[j, 32:48, :] = tail.astype(BF16)
                send(ret_send.at[j], ret_in.at[head], ret_ss.at[0], ret_rs.at[head], 2 * j + core)

    @pl.when(is_far)
    def _():
        qf = qz[...]
        limit = iota((TOK, 128), 1) - iota((TOK, 128), 0)
        far_m[...] = jnp.full((1, 128), NEG, F32)
        far_o[...] = jnp.zeros((128, 128), F32)

        def slab(n):
            z = jnp.where(zh > 1, jnp.where(n == 0, 0, zh - n + 1), zh - n)

            def wait(b):
                @pl.when(b % 4 != gx)
                def _():
                    arrived(kvx.at[b], blk_rs.at[b])
            loop(4 * z, jnp.minimum(4 * z + 4, g), wait)
            part = kvx[pl.ds(4 * z, 4)].reshape(TOK, 128)
            x = jnp.where(limit >= TOK * z - 128 * g, nt(part, qf), NEG)
            old = far_m[...]
            new = jnp.maximum(old, jnp.max(x, axis=0, keepdims=True))
            xt = jnp.where(row_v, 1.0, nt(eye, part)).astype(BF16)
            y = nn(xt, jnp.exp2((x - new) * C).astype(BF16))
            far_o[...] = far_o[...] * jnp.exp2((old - new) * C) + y
            far_m[...] = new
        loop(0, zh + 1, slab)
        m, o = far_m[...], far_o[...]
        total = o[0:1]
        norm = (o[64:128] / total).astype(BF16)
        ls = three(m * C + jnp.log(total) * math.log2(math.e))
        r = iota((64, 128), 0)
        tail = jnp.where(r == 0, ls[0], jnp.where(r == 1, ls[1], jnp.where(r == 2, ls[2], 0.0)))
        both = jnp.concatenate([norm, tail.astype(BF16)], axis=0)
        i, j = iota((TOK, 128), 0), iota((TOK, 128), 1)
        place = onehot((j == 4 * (i // 16) + i % 16) & (i % 16 < 4))
        fret_send[...] = nt(place, both).astype(BF16).reshape(SEQ, 16, 128)
        loop(0, SEQ, lambda i: send(fret_send.at[i], fret_in.at[head], ret_ss.at[1], fret_rs.at[head], i))

    tok = iota((1, TOK), 1)
    low48 = iota((48, 128), 1) < HD
    zero = jnp.zeros((), BF16)
    for h in range(HEADS):
        arrived(ret_in.at[h], ret_rs.at[h])
        x = ret_in[h]
        left = jnp.concatenate([jnp.where(low48, x, zero), jnp.where(low, zero, x[0:32])], axis=0)
        u = nn(left, spread[h])
        l1 = jnp.where(tok % 8 == off_ref[0, h], u[32:33] + u[33:34] + u[34:35], NEG)
        m0 = top[h]
        big = jnp.maximum(m0, l1)
        w0, w1 = jnp.exp2(m0 - big), jnp.exp2(l1 - big)
        top[h] = big
        tot[h] = w0 * tot[h] + w1
        for a in range(2):
            rows = slice(64 * h + 32 * a, 64 * h + 32 * a + 32)
            acc[rows, :] = acc[rows, :] * w0 + u[48 * a:48 * a + 32] * w1
    for h in range(HEADS):
        arrived(fret_in.at[h], fret_rs.at[h])
        w = tn(fret_in[h], far_hot[h])
        l2 = jnp.where(tok % 128 == off_ref[1, h], w[64:65] + w[65:66] + w[66:67], NEG)
        m0 = top[h]
        big = jnp.maximum(m0, l2)
        w0, w2 = jnp.exp2(m0 - big), jnp.exp2(l2 - big)
        inv = 1.0 / (w0 * tot[h] + w2)
        rows = slice(64 * h, 64 * h + 64)
        out_ref[rows, :] = (acc[rows, :] * (w0 * inv) + w[0:64] * (w2 * inv)).astype(BF16)

    sent(n_send.at[:, pl.ds(0, 64)], out_ss.at[2])

    @pl.when(zh == 2)
    def _():
        sent(f_send, out_ss.at[3])

    @pl.when(is_near)
    def _():
        sent(n_send.at[pl.ds(0, HEADS - 1)], out_ss.at[1])
        sent(ret_send.at[pl.ds(0, 15)], ret_ss.at[0])

    @pl.when(jnp.logical_not(is_near))
    def _():
        sent(n_send, out_ss.at[1])

    @pl.when(is_far)
    def _():
        sent(f_send.at[pl.ds(0, HEADS - 1)], out_ss.at[0])
        sent(fret_send.at[pl.ds(0, SEQ - 1)], ret_ss.at[1])
        for i in range(1, 4):
            @pl.when(gx + i < 4)
            def _():
                on_x(g, i).wait_send()

            loop(0, zh, lambda z: on_x(4 * z + gx, i).wait_send())

        @pl.when(zh < 2)
        def _():
            for i in range(2):
                on_z(i).wait_send()

        @pl.when(zh == 1)
        def _():
            on_z_pass().wait_send()

    @pl.when(jnp.logical_not(is_far))
    def _():
        sent(f_send, out_ss.at[0])


def on_device(queries, keys, values, offsets, out_weight):
    hbm = pl.BlockSpec(memory_space=pltpu.HBM)
    vm = pltpu.VMEM
    dma = pltpu.SemaphoreType.DMA
    merged = pl.pallas_call(
        kernel,
        out_shape=jax.ShapeDtypeStruct((HEADS * HD, TOK), BF16),
        in_specs=[hbm, hbm, hbm, hbm],
        out_specs=pl.BlockSpec(memory_space=pltpu.VMEM),
        scratch_shapes=[
            vm((TOK, HEADS * HD), BF16),
            vm((TOK, HEADS * HD), BF16),
            vm((TOK, HEADS * HD), BF16),
            pltpu.SMEM((2, HEADS), jnp.int32),
            vm((HEADS, 96, 128), BF16),
            vm((HEADS, 16, 128), BF16),
            vm((16, 96, 128), BF16),
            vm((16, 64, 128), BF16),
            vm((SEQ, 16, 128), BF16),
            vm((SEQ, 16, 128), BF16),
            vm((128, 128), BF16),
            vm((8, 128, 256), BF16),
            vm((8, 256, 256), F32),
            vm((16, 48, 128), BF16),
            vm((HEADS, 48, 128), BF16),
            vm((GRP, 128, 128), BF16),
            vm((SEQ, 16, 128), BF16),
            vm((HEADS, 16, 128), BF16),
            vm((HEADS * HD, TOK), F32),
            vm((HEADS, 1, TOK), F32),
            vm((HEADS, 1, TOK), F32),
            vm((HEADS, 128, TOK), BF16),
            vm((HEADS, 16, TOK), BF16),
            vm((1, 128), F32),
            vm((128, 128), F32),
            dma((4,)), dma((4,)), dma((4,)), dma((4,)), dma, dma,
            dma((3,)), dma((4, 3)), dma((GRP,)),
            pltpu.SemaphoreType.REGULAR,
            dma((2,)), dma((HEADS,)), dma((HEADS,)),
        ],
        compiler_params=pltpu.CompilerParams(
            collective_id=0, has_side_effects=True, vmem_limit_bytes=55783424
        ),
    )(queries, keys, values, offsets)
    return tn(merged, out_weight).astype(BF16)


def solution(mesh):
    placed = (P(("grp", "seq"), None), P(("grp", "seq"), None), P(("grp", "seq"), None), P(), P())
    return jax.shard_map(
        on_device, mesh=mesh, in_specs=placed, out_specs=P(("grp", "seq"), None), check_vma=False
    )
```

```python
import math

import jax
import jax.numpy as jnp
from jax import lax
from jax.experimental import pallas as pl
from jax.experimental.pallas import tpu as pltpu
from jax.sharding import PartitionSpec as P

MESH = pl.DeviceIdType.MESH
HEADS = 6
HD = 64
TOK = 512
SEQ = 32
GRP = 16
NEG = -1e30
C = math.log2(math.e) / math.sqrt(HD)
F32 = jnp.float32
BF16 = jnp.bfloat16


def nt(a, b):
    return lax.dot_general(a, b, (((1,), (1,)), ((), ())), preferred_element_type=F32)


def nn(a, b):
    return lax.dot_general(a, b, (((1,), (0,)), ((), ())), preferred_element_type=F32)


def tn(a, b):
    return lax.dot_general(a, b, (((0,), (0,)), ((), ())), preferred_element_type=F32)


def iota(shape, dim):
    return lax.broadcasted_iota(jnp.int32, shape, dim)


def onehot(cond):
    return jnp.where(cond, 1.0, 0.0).astype(BF16)


def near_chip(h):
    return (5 * h + 1) % 16


def far_chip(h):
    return (5 * (h + 6) + 1) % 16


def turn(x):
    return pltpu.roll(x, HD, 1)


def three(x):
    hi = x.astype(BF16).astype(F32)
    rest = x - hi
    mid = rest.astype(BF16).astype(F32)
    return hi, mid, rest - mid


def loop(lo, hi, f):
    def step(i, c):
        f(i)
        return c

    lax.fori_loop(lo, hi, step, 0)


def kernel(
    q_hbm, k_hbm, v_hbm, off_hbm, out_ref,
    q_ref, k_ref, v_ref, off_ref,
    n_send, f_send, n_in, o_in, f_in, g_in, qz, kvt, scr, ret_send, ret_in,
    kvx, fret_send, fret_in, acc, top, tot, spread, far_hot, far_m, far_o, place,
    in_sem, out_ss, n_rs, o_rs, f_rs, g_rs, z_ss, x_ss, blk_rs, go, ret_ss, ret_rs, fret_rs,
):
    s = lax.axis_index("seq")
    g = lax.axis_index("grp")
    chip, core = s // 2, s % 2
    zh, gx = g // 4, g % 4
    role = ((chip + 15) * 13) % 16
    is_near = role < HEADS
    on_far = (role >= HEADS) & (role < 2 * HEADS)
    is_far = on_far & (core == 0)
    head = role % HEADS
    sibling = s + 1 - 2 * core

    inputs = [
        pltpu.make_async_copy(src, dst, in_sem.at[i])
        for i, (src, dst) in enumerate(
            ((off_hbm, off_ref), (q_hbm, q_ref), (k_hbm, k_ref), (v_hbm, v_ref))
        )
    ]
    for c in inputs:
        c.start()

    barrier = pltpu.get_barrier_semaphore()

    def far_seat(i):
        part = ((i // 2 + 15) * 13) % 16
        return (part >= HEADS) & (part < 2 * HEADS) & (i % 2 == 0) & (zh < 2)

    def hello(axis, target):
        pl.semaphore_signal(barrier, inc=1, device_id={axis: target}, device_id_type=MESH)

    @pl.when(is_far)
    def _():
        for i in range(1, 4):
            pl.semaphore_signal(
                barrier, inc=1, device_id={"grp": 4 * zh + (gx + i) % 4, "seq": sibling}, device_id_type=MESH
            )

        @pl.when((zh == 1) | (zh == 2))
        def _():
            hello("grp", g - 4)

        @pl.when(zh == 3)
        def _():
            hello("grp", g - 12)
            hello("grp", g - 8)

            loop(0, SEQ, lambda i: pl.semaphore_signal(
                barrier, inc=1, device_id={"grp": g - 4, "seq": i}, device_id_type=MESH
            ))

    @pl.when(is_near | is_far)
    def _():
        def step(i):
            @pl.when((i != s) & jnp.logical_not(far_seat(i)))
            def _():
                hello("seq", i)
        loop(0, SEQ, step)

    low = iota((32, 128), 1) < HD
    low16 = iota((16, 128), 1) < HD
    row16 = iota((16, 128), 0)
    near_diff = iota((32, 256), 1) - 8 * iota((32, 256), 0)
    fr = iota((16, TOK), 0)
    far_diff = jnp.where(fr < 8, iota((16, TOK), 1) - 128 * (fr % 4), -1)
    for c in inputs:
        c.wait()
    for p in range(3):
        near_hot = [onehot(near_diff == off_ref[0, 2 * p + e]) for e in range(2)]
        hot = [onehot(far_diff == off_ref[1, 2 * p + e]) for e in range(2)]
        for e in range(2):
            far_hot[2 * p + e] = hot[e]
        picked = []
        for ref in (q_ref, k_ref, v_ref):
            halves = []
            for a in range(2):
                left = jnp.concatenate(near_hot + [f[:, 256 * a:256 * a + 256] for f in hot], axis=0)
                halves.append(nn(left, ref[256 * a:256 * a + 256, 128 * p:128 * p + 128]))
            picked.append(halves)
        pq, pk, pv = picked
        for e in range(2):
            h = 2 * p + e
            for a in range(2):
                rk, rv = pk[a][32 * e:32 * e + 32], pv[a][32 * e:32 * e + 32]
                kv = jnp.where(low, rk, turn(rv)) if e == 0 else jnp.where(low, turn(rk), rv)
                n_send[h, 32 * a:32 * a + 32, :] = kv.astype(BF16)
            r0, r1 = pq[0][32 * e:32 * e + 32], pq[1][32 * e:32 * e + 32]
            qq = jnp.where(low, r0, turn(r1)) if e == 0 else jnp.where(low, turn(r0), r1)
            n_send[h, 64:96, :] = qq.astype(BF16)
            lo = 64 + 16 * e
            fq, fk, fv = [x[0][lo:lo + 16] + x[1][lo:lo + 16] for x in (pq, pk, pv)]
            if e == 0:
                fkv, fqz = jnp.where(low16, fk, turn(fv)), fq
            else:
                fkv, fqz = jnp.where(low16, turn(fk), fv), turn(fq)
            tile = jnp.where(row16 < 4, fkv, jnp.where(low16 & (row16 < 8), fqz, 0.0))
            f_send[h] = tile.astype(BF16)

    ahead = jnp.where(zh == 2, HEADS, 0)

    @pl.when(is_near | (is_far & (zh > 1)))
    def _():
        pl.semaphore_wait(barrier, 3 * HEADS - 1 + ahead)

    @pl.when(jnp.logical_not(is_near | on_far))
    def _():
        pl.semaphore_wait(barrier, 3 * HEADS + ahead)

    @pl.when(on_far & (core == 1))
    def _():
        pl.semaphore_wait(barrier, 3 * HEADS + 3 + ahead)
        pl.semaphore_signal(go, inc=1, device_id={"seq": sibling}, device_id_type=MESH)

    @pl.when(is_far & (zh < 2))
    def _():
        pl.semaphore_wait(go, 1)

    def copy(src, dst, ss, rs, target, axis="seq"):
        return pltpu.make_async_remote_copy(
            src_ref=src, dst_ref=dst, send_sem=ss, recv_sem=rs, device_id={axis: target}, device_id_type=MESH
        )

    def send(src, dst, ss, rs, target):
        @pl.when(s == target)
        def _():
            pltpu.make_async_copy(src, dst, rs).start()

        @pl.when(s != target)
        def _():
            copy(src, dst, ss, rs, target).start()

    def arrived(dst, rs):
        copy(dst, dst, in_sem.at[0], rs, sibling).wait_recv()

    def sent(src, ss):
        copy(src, src, ss, in_sem.at[0], sibling).wait_send()

    for i in range(HEADS):
        h = (chip + i) % HEADS
        send(f_send.at[h], f_in.at[s], out_ss.at[0], f_rs, 2 * far_chip(h))
    def early(h):
        return pltpu.make_async_remote_copy(
            src_ref=f_send.at[h], dst_ref=g_in.at[s], send_sem=out_ss.at[3], recv_sem=g_rs,
            device_id={"grp": g + 4, "seq": 2 * far_chip(h)}, device_id_type=MESH,
        )

    @pl.when(zh == 2)
    def _():
        for i in range(HEADS):
            early((chip + i) % HEADS).start()

    for i in range(HEADS):
        h = (chip + i) % HEADS
        send(n_send.at[h], n_in.at[chip], out_ss.at[1], n_rs.at[chip // 4], 2 * near_chip(h) + core)
    for i in range(HEADS):
        h = (chip + i) % HEADS
        copy(
            n_send.at[h, pl.ds(0, 64)], o_in.at[chip], out_ss.at[2], o_rs.at[chip // 4], 2 * near_chip(h) + 1 - core
        ).start()

    eye = onehot(iota((128, 128), 0) == iota((128, 128), 1))
    causal = iota((256, 256), 0) <= iota((256, 256), 1)
    lane_q = iota((TOK, 128), 1) < HD
    row_v = iota((128, TOK), 0) < HD
    row_one = iota((128, 256), 0) < HD

    def local_pair(p):
        cols = slice(128 * p, 128 * p + 128)
        kp, qp, vp = k_ref[:, cols], q_ref[:, cols], v_ref[:, cols]
        vt = nt(eye, vp)
        for e in range(2):
            h = 2 * p + e
            mine = lane_q if e == 0 else jnp.logical_not(lane_q)
            qe = jnp.where(mine, qp, jnp.zeros((), BF16))
            mine_v = row_v if e == 0 else jnp.logical_not(row_v)
            ve = jnp.where(mine_v, vt, 1.0).astype(BF16)
            for t in range(2):
                qt = qe[256 * t:256 * t + 256]
                parts = [nt(kp[256 * b:256 * b + 256], qt) for b in range(t + 1)]
                parts[t] = jnp.where(causal, parts[t], NEG)
                m = jnp.max(parts[0], axis=0, keepdims=True)
                for x in parts[1:]:
                    m = jnp.maximum(m, jnp.max(x, axis=0, keepdims=True))
                o = None
                for b, x in enumerate(parts):
                    w = jnp.exp2((x - m) * C).astype(BF16)
                    y = nn(ve[:, 256 * b:256 * b + 256], w)
                    o = y if o is None else o + y
                ts = slice(256 * t, 256 * t + 256)
                acc[64 * h:64 * h + 64, ts] = o[64 * e:64 * e + 64]
                other = 64 * (1 - e)
                tot[h, :, ts] = o[other:other + 1]
                top[h, :, ts] = m * C

    def to_group(b, ss, i):
        return copy(kvx.at[b], kvx.at[b], ss, blk_rs.at[b], i, "grp")

    def on_z(i):
        return to_group(g, z_ss.at[i], jnp.where((zh == 0) & (i == 1), g + 12, g + 4 + 4 * i))

    def on_z_pass():
        return to_group(gx, z_ss.at[2], g + 4)

    def on_x(b, i):
        return to_group(b, x_ss.at[b // 4, i - 1], 4 * zh + (gx + i) % 4)

    for p in range(3):
        local_pair(p)

    @pl.when(is_far)
    def _():
        def clear(b):
            kvx[b] = jnp.zeros((128, 128), BF16)
        loop(g + 1, 4 * zh + 4, clear)
        arrived(f_in, f_rs)
        i, j = iota((128, TOK), 0), iota((128, TOK), 1)
        base = 16 * (i // 4) + i % 4
        keys = onehot(j == base)
        rows = f_in[...].reshape(TOK, 128)
        kvx[g] = nn(keys, rows).astype(BF16)
        qz[...] = nn(onehot(j == base + 4), rows).astype(BF16)

        @pl.when(zh > 1)
        def _():
            pl.semaphore_wait(go, 1)
        for i in range(1, 4):
            @pl.when(gx + i < 4)
            def _():
                on_x(g, i).start()

        @pl.when(zh < 2)
        def _():
            pl.semaphore_wait(barrier, 2)
            for i in (1, 0):
                on_z(i).start()

        @pl.when(zh == 3)
        def _():
            arrived(g_in, g_rs)
            kvx[g - 4] = nn(keys, g_in[...].reshape(TOK, 128)).astype(BF16)
            for i in range(1, 4):
                on_x(g - 4, i).start()

        def passing(z):
            b = 4 * z + gx
            arrived(kvx.at[b], blk_rs.at[b])

            @pl.when(zh == 1)
            def _():
                on_z_pass().start()
            for i in range(1, 4):
                on_x(b, i).start()
        loop(0, jnp.minimum(zh, 2), passing)

    for h in range(HEADS):
        spread[h] = onehot(iota((128, TOK), 1) - 8 * (iota((128, TOK), 0) % 64) == off_ref[0, h])

    @pl.when(is_near)
    def _():
        inner = iota((256, 256), 0) // 64 < iota((256, 256), 1) // 64 + core
        for t in range(4):
            arrived(n_in.at[pl.ds(4 * t, 4)], n_rs.at[t])
            arrived(o_in.at[pl.ds(4 * t, 4)], o_rs.at[t])

            def part(b, side):
                x = n_in[4 * b:4 * b + 4, 0:64, :] if side == 0 else o_in[4 * b:4 * b + 4]
                return x.reshape(256, 128)

            for side in range(2):
                x = nt(eye, part(t, side))
                kvt[2 * t + side] = jnp.where(row_one, 1.0, x).astype(BF16)
            asks = []
            for i in range(4 * t, 4 * t + 4):
                x = n_in[i, 64:96, :].astype(F32)
                asks += [jnp.where(low, x, 0.0), jnp.where(low, turn(x), 0.0)]
            qt = jnp.concatenate(asks, axis=0).astype(BF16)
            m = None
            for n in range(2 * t + 2):
                x = nt(part(n // 2, n % 2), qt)
                if n // 2 == t:
                    x = jnp.where(causal if n % 2 == 0 else inner, x, NEG)
                scr[n] = x
                y = jnp.max(x, axis=0, keepdims=True)
                m = y if m is None else jnp.maximum(m, y)
            o = None
            for n in range(2 * t + 2):
                w = jnp.exp2((scr[n] - m) * C).astype(BF16)
                y = nn(kvt[n], w)
                o = y if o is None else o + y
            total = o[0:1]
            norm = o[64:128] / total
            lses = three(m * C + jnp.log(total) * math.log2(math.e))
            for jj in range(4):
                j = 4 * t + jj
                cols = slice(128 * (jj // 2), 128 * (jj // 2) + 128)
                top_half, bottom = norm[0:32, cols], norm[32:64, cols]
                ls = [x[:, cols] for x in lses]
                if jj % 2 == 0:
                    packed = jnp.where(low, top_half, turn(bottom))
                else:
                    packed = jnp.where(low, turn(top_half), bottom)
                tail = jnp.where(row16 == 0, ls[0], jnp.where(row16 == 1, ls[1], jnp.where(row16 == 2, ls[2], 0.0)))
                if jj % 2 == 1:
                    tail = turn(tail)
                ret_send[j, 0:32, :] = packed.astype(BF16)
                ret_send[j, 32:48, :] = tail.astype(BF16)
                send(ret_send.at[j], ret_in.at[head], ret_ss.at[0], ret_rs.at[head], 2 * j + core)

    @pl.when(is_far)
    def _():
        i, j = iota((TOK, 128), 0), iota((TOK, 128), 1)
        place[...] = onehot((j == 4 * (i // 16) + i % 16) & (i % 16 < 4))
        qf = qz[...]
        limit = iota((TOK, 128), 1) - iota((TOK, 128), 0)
        far_m[...] = jnp.full((1, 128), NEG, F32)
        far_o[...] = jnp.zeros((128, 128), F32)

        def slab(n):
            z = jnp.where(zh > 1, jnp.where(n == 0, 0, zh - n + 1), zh - n)

            def wait(b):
                @pl.when(b % 4 != gx)
                def _():
                    arrived(kvx.at[b], blk_rs.at[b])
            loop(4 * z, jnp.minimum(4 * z + 4, g), wait)
            part = kvx[pl.ds(4 * z, 4)].reshape(TOK, 128)
            x = jnp.where(limit >= TOK * z - 128 * g, nt(part, qf), NEG)
            old = far_m[...]
            new = jnp.maximum(old, jnp.max(x, axis=0, keepdims=True))
            xt = jnp.where(row_v, 1.0, nt(eye, part)).astype(BF16)
            y = nn(xt, jnp.exp2((x - new) * C).astype(BF16))
            far_o[...] = far_o[...] * jnp.exp2((old - new) * C) + y
            far_m[...] = new
        loop(0, zh + 1, slab)
        m, o = far_m[...], far_o[...]
        total = o[0:1]
        norm = (o[64:128] / total).astype(BF16)
        ls = three(m * C + jnp.log(total) * math.log2(math.e))
        r = iota((64, 128), 0)
        tail = jnp.where(r == 0, ls[0], jnp.where(r == 1, ls[1], jnp.where(r == 2, ls[2], 0.0)))
        both = jnp.concatenate([norm, tail.astype(BF16)], axis=0)
        fret_send[...] = nt(place[...], both).astype(BF16).reshape(SEQ, 16, 128)
        loop(0, SEQ, lambda i: send(fret_send.at[i], fret_in.at[head], ret_ss.at[1], fret_rs.at[head], i))

    tok = iota((1, TOK), 1)
    low48 = iota((48, 128), 1) < HD
    zero = jnp.zeros((), BF16)
    for h in range(HEADS):
        arrived(ret_in.at[h], ret_rs.at[h])
        x = ret_in[h]
        left = jnp.concatenate([jnp.where(low48, x, zero), jnp.where(low, zero, x[0:32])], axis=0)
        u = nn(left, spread[h])
        l1 = jnp.where(tok % 8 == off_ref[0, h], u[32:33] + u[33:34] + u[34:35], NEG)
        m0 = top[h]
        big = jnp.maximum(m0, l1)
        w0, w1 = jnp.exp2(m0 - big), jnp.exp2(l1 - big)
        top[h] = big
        tot[h] = w0 * tot[h] + w1
        for a in range(2):
            rows = slice(64 * h + 32 * a, 64 * h + 32 * a + 32)
            acc[rows, :] = acc[rows, :] * w0 + u[48 * a:48 * a + 32] * w1
    for h in range(HEADS):
        arrived(fret_in.at[h], fret_rs.at[h])
        w = tn(fret_in[h], far_hot[h])
        l2 = jnp.where(tok % 128 == off_ref[1, h], w[64:65] + w[65:66] + w[66:67], NEG)
        m0 = top[h]
        big = jnp.maximum(m0, l2)
        w0, w2 = jnp.exp2(m0 - big), jnp.exp2(l2 - big)
        inv = 1.0 / (w0 * tot[h] + w2)
        rows = slice(64 * h, 64 * h + 64)
        out_ref[rows, :] = (acc[rows, :] * (w0 * inv) + w[0:64] * (w2 * inv)).astype(BF16)

    sent(n_send.at[:, pl.ds(0, 64)], out_ss.at[2])

    @pl.when(zh == 2)
    def _():
        sent(f_send, out_ss.at[3])

    @pl.when(is_near)
    def _():
        sent(n_send.at[pl.ds(0, HEADS - 1)], out_ss.at[1])
        sent(ret_send.at[pl.ds(0, 15)], ret_ss.at[0])

    @pl.when(jnp.logical_not(is_near))
    def _():
        sent(n_send, out_ss.at[1])

    @pl.when(is_far)
    def _():
        sent(f_send.at[pl.ds(0, HEADS - 1)], out_ss.at[0])
        sent(fret_send.at[pl.ds(0, SEQ - 1)], ret_ss.at[1])
        for i in range(1, 4):
            @pl.when(gx + i < 4)
            def _():
                on_x(g, i).wait_send()

            loop(0, zh, lambda z: on_x(4 * z + gx, i).wait_send())

        @pl.when(zh < 2)
        def _():
            for i in range(2):
                on_z(i).wait_send()

        @pl.when(zh == 1)
        def _():
            on_z_pass().wait_send()

    @pl.when(jnp.logical_not(is_far))
    def _():
        sent(f_send, out_ss.at[0])


def on_device(queries, keys, values, offsets, out_weight):
    hbm = pl.BlockSpec(memory_space=pltpu.HBM)
    vm = pltpu.VMEM
    dma = pltpu.SemaphoreType.DMA
    merged = pl.pallas_call(
        kernel,
        out_shape=jax.ShapeDtypeStruct((HEADS * HD, TOK), BF16),
        in_specs=[hbm, hbm, hbm, hbm],
        out_specs=pl.BlockSpec(memory_space=pltpu.VMEM),
        scratch_shapes=[
            vm((TOK, HEADS * HD), BF16),
            vm((TOK, HEADS * HD), BF16),
            vm((TOK, HEADS * HD), BF16),
            pltpu.SMEM((2, HEADS), jnp.int32),
            vm((HEADS, 96, 128), BF16),
            vm((HEADS, 16, 128), BF16),
            vm((16, 96, 128), BF16),
            vm((16, 64, 128), BF16),
            vm((SEQ, 16, 128), BF16),
            vm((SEQ, 16, 128), BF16),
            vm((128, 128), BF16),
            vm((8, 128, 256), BF16),
            vm((8, 256, 256), F32),
            vm((16, 48, 128), BF16),
            vm((HEADS, 48, 128), BF16),
            vm((GRP, 128, 128), BF16),
            vm((SEQ, 16, 128), BF16),
            vm((HEADS, 16, 128), BF16),
            vm((HEADS * HD, TOK), F32),
            vm((HEADS, 1, TOK), F32),
            vm((HEADS, 1, TOK), F32),
            vm((HEADS, 128, TOK), BF16),
            vm((HEADS, 16, TOK), BF16),
            vm((1, 128), F32),
            vm((128, 128), F32),
            vm((TOK, 128), BF16),
            dma((4,)), dma((4,)), dma((4,)), dma((4,)), dma, dma,
            dma((3,)), dma((4, 3)), dma((GRP,)),
            pltpu.SemaphoreType.REGULAR,
            dma((2,)), dma((HEADS,)), dma((HEADS,)),
        ],
        compiler_params=pltpu.CompilerParams(
            collective_id=0, has_side_effects=True, vmem_limit_bytes=55783424
        ),
    )(queries, keys, values, offsets)
    return tn(merged, out_weight).astype(BF16)


def solution(mesh):
    placed = (P(("grp", "seq"), None), P(("grp", "seq"), None), P(("grp", "seq"), None), P(), P())
    return jax.shard_map(
        on_device, mesh=mesh, in_specs=placed, out_specs=P(("grp", "seq"), None), check_vma=False
    )
```

```python
import math

import jax
import jax.numpy as jnp
from jax import lax
from jax.experimental import pallas as pl
from jax.experimental.pallas import tpu as pltpu
from jax.sharding import PartitionSpec as P

MESH = pl.DeviceIdType.MESH
HEADS = 6
HD = 64
TOK = 512
SEQ = 32
GRP = 16
NEG = -1e30
C = math.log2(math.e) / math.sqrt(HD)
F32 = jnp.float32
BF16 = jnp.bfloat16


def nt(a, b):
    return lax.dot_general(a, b, (((1,), (1,)), ((), ())), preferred_element_type=F32)


def nn(a, b):
    return lax.dot_general(a, b, (((1,), (0,)), ((), ())), preferred_element_type=F32)


def tn(a, b):
    return lax.dot_general(a, b, (((0,), (0,)), ((), ())), preferred_element_type=F32)


def iota(shape, dim):
    return lax.broadcasted_iota(jnp.int32, shape, dim)


def onehot(cond):
    return jnp.where(cond, 1.0, 0.0).astype(BF16)


def near_chip(h):
    return (5 * h + 1) % 16


def far_chip(h):
    return (5 * (h + 6) + 1) % 16


def turn(x):
    return pltpu.roll(x, HD, 1)


def three(x):
    hi = x.astype(BF16).astype(F32)
    rest = x - hi
    mid = rest.astype(BF16).astype(F32)
    return hi, mid, rest - mid


def loop(lo, hi, f):
    def step(i, c):
        f(i)
        return c

    lax.fori_loop(lo, hi, step, 0)


def kernel(
    q_hbm, k_hbm, v_hbm, off_hbm, out_ref,
    q_ref, k_ref, v_ref, off_ref,
    n_send, f_send, n_in, o_in, f_in, g_in, qz, kvt, scr, ret_send, ret_in,
    kvx, fret_send, fret_in, acc, top, tot, spread, far_hot, far_m, far_o,
    in_sem, out_ss, n_rs, o_rs, f_rs, g_rs, z_ss, x_ss, blk_rs, go, ret_ss, ret_rs, fret_rs,
):
    s = lax.axis_index("seq")
    g = lax.axis_index("grp")
    chip, core = s // 2, s % 2
    zh, gx = g // 4, g % 4
    role = ((chip + 15) * 13) % 16
    is_near = role < HEADS
    on_far = (role >= HEADS) & (role < 2 * HEADS)
    is_far = on_far & (core == 0)
    head = role % HEADS
    sibling = s + 1 - 2 * core

    inputs = [
        pltpu.make_async_copy(src, dst, in_sem.at[i])
        for i, (src, dst) in enumerate(
            ((off_hbm, off_ref), (q_hbm, q_ref), (k_hbm, k_ref), (v_hbm, v_ref))
        )
    ]
    for c in inputs:
        c.start()

    barrier = pltpu.get_barrier_semaphore()

    def far_seat(i):
        part = ((i // 2 + 15) * 13) % 16
        return (part >= HEADS) & (part < 2 * HEADS) & (i % 2 == 0) & (zh < 2)

    def hello(axis, target):
        pl.semaphore_signal(barrier, inc=1, device_id={axis: target}, device_id_type=MESH)

    @pl.when(is_far)
    def _():
        for i in range(1, 4):
            pl.semaphore_signal(
                barrier, inc=1, device_id={"grp": 4 * zh + (gx + i) % 4, "seq": sibling}, device_id_type=MESH
            )

        @pl.when((zh == 1) | (zh == 2))
        def _():
            hello("grp", g - 4)

        @pl.when(zh == 3)
        def _():
            hello("grp", g - 12)
            hello("grp", g - 8)

            loop(0, SEQ, lambda i: pl.semaphore_signal(
                barrier, inc=1, device_id={"grp": g - 4, "seq": i}, device_id_type=MESH
            ))

    @pl.when(is_near | is_far)
    def _():
        def step(i):
            @pl.when((i != s) & jnp.logical_not(far_seat(i)))
            def _():
                hello("seq", i)
        loop(0, SEQ, step)

    low = iota((32, 128), 1) < HD
    low16 = iota((16, 128), 1) < HD
    row16 = iota((16, 128), 0)
    near_diff = iota((32, 256), 1) - 8 * iota((32, 256), 0)
    fr = iota((16, TOK), 0)
    far_diff = jnp.where(fr < 8, iota((16, TOK), 1) - 128 * (fr % 4), -1)
    for c in inputs:
        c.wait()
    for p in range(3):
        near_hot = [onehot(near_diff == off_ref[0, 2 * p + e]) for e in range(2)]
        hot = [onehot(far_diff == off_ref[1, 2 * p + e]) for e in range(2)]
        for e in range(2):
            far_hot[2 * p + e] = hot[e]
        picked = []
        for ref in (q_ref, k_ref, v_ref):
            halves = []
            for a in range(2):
                left = jnp.concatenate(near_hot + [f[:, 256 * a:256 * a + 256] for f in hot], axis=0)
                halves.append(nn(left, ref[256 * a:256 * a + 256, 128 * p:128 * p + 128]))
            picked.append(halves)
        pq, pk, pv = picked
        for e in range(2):
            h = 2 * p + e
            for a in range(2):
                rk, rv = pk[a][32 * e:32 * e + 32], pv[a][32 * e:32 * e + 32]
                kv = jnp.where(low, rk, turn(rv)) if e == 0 else jnp.where(low, turn(rk), rv)
                n_send[h, 32 * a:32 * a + 32, :] = kv.astype(BF16)
            r0, r1 = pq[0][32 * e:32 * e + 32], pq[1][32 * e:32 * e + 32]
            qq = jnp.where(low, r0, turn(r1)) if e == 0 else jnp.where(low, turn(r0), r1)
            n_send[h, 64:96, :] = qq.astype(BF16)
            lo = 64 + 16 * e
            fq, fk, fv = [x[0][lo:lo + 16] + x[1][lo:lo + 16] for x in (pq, pk, pv)]
            if e == 0:
                fkv, fqz = jnp.where(low16, fk, turn(fv)), fq
            else:
                fkv, fqz = jnp.where(low16, turn(fk), fv), turn(fq)
            tile = jnp.where(row16 < 4, fkv, jnp.where(low16 & (row16 < 8), fqz, 0.0))
            f_send[h] = tile.astype(BF16)

    ahead = jnp.where(zh == 2, HEADS, 0)

    @pl.when(is_near | (is_far & (zh > 1)))
    def _():
        pl.semaphore_wait(barrier, 3 * HEADS - 1 + ahead)

    @pl.when(jnp.logical_not(is_near | on_far))
    def _():
        pl.semaphore_wait(barrier, 3 * HEADS + ahead)

    @pl.when(on_far & (core == 1))
    def _():
        pl.semaphore_wait(barrier, 3 * HEADS + 3 + ahead)
        pl.semaphore_signal(go, inc=1, device_id={"seq": sibling}, device_id_type=MESH)

    @pl.when(is_far & (zh < 2))
    def _():
        pl.semaphore_wait(go, 1)

    def copy(src, dst, ss, rs, target, axis="seq"):
        return pltpu.make_async_remote_copy(
            src_ref=src, dst_ref=dst, send_sem=ss, recv_sem=rs, device_id={axis: target}, device_id_type=MESH
        )

    def send(src, dst, ss, rs, target):
        @pl.when(s == target)
        def _():
            pltpu.make_async_copy(src, dst, rs).start()

        @pl.when(s != target)
        def _():
            copy(src, dst, ss, rs, target).start()

    def arrived(dst, rs):
        copy(dst, dst, in_sem.at[0], rs, sibling).wait_recv()

    def sent(src, ss):
        copy(src, src, ss, in_sem.at[0], sibling).wait_send()

    for i in range(HEADS):
        h = (chip + i) % HEADS
        send(f_send.at[h], f_in.at[s], out_ss.at[0], f_rs, 2 * far_chip(h))
    def early(h):
        return pltpu.make_async_remote_copy(
            src_ref=f_send.at[h], dst_ref=g_in.at[s], send_sem=out_ss.at[3], recv_sem=g_rs,
            device_id={"grp": g + 4, "seq": 2 * far_chip(h)}, device_id_type=MESH,
        )

    @pl.when(zh == 2)
    def _():
        for i in range(HEADS):
            early((chip + i) % HEADS).start()

    for i in range(HEADS):
        h = (chip + i) % HEADS
        send(n_send.at[h], n_in.at[chip], out_ss.at[1], n_rs.at[chip // 4], 2 * near_chip(h) + core)
    for i in range(HEADS):
        h = (chip + i) % HEADS
        copy(
            n_send.at[h, pl.ds(0, 64)], o_in.at[chip], out_ss.at[2], o_rs.at[chip // 4], 2 * near_chip(h) + 1 - core
        ).start()

    eye = onehot(iota((128, 128), 0) == iota((128, 128), 1))
    causal = iota((256, 256), 0) <= iota((256, 256), 1)
    lane_q = iota((TOK, 128), 1) < HD
    row_v = iota((128, TOK), 0) < HD
    row_one = iota((128, 256), 0) < HD

    def local_pair(p):
        cols = slice(128 * p, 128 * p + 128)
        kp, qp, vp = k_ref[:, cols], q_ref[:, cols], v_ref[:, cols]
        vt = nt(eye, vp)
        for e in range(2):
            h = 2 * p + e
            mine = lane_q if e == 0 else jnp.logical_not(lane_q)
            qe = jnp.where(mine, qp, jnp.zeros((), BF16))
            mine_v = row_v if e == 0 else jnp.logical_not(row_v)
            ve = jnp.where(mine_v, vt, 1.0).astype(BF16)
            for t in range(2):
                qt = qe[256 * t:256 * t + 256]
                parts = [nt(kp[256 * b:256 * b + 256], qt) for b in range(t + 1)]
                parts[t] = jnp.where(causal, parts[t], NEG)
                m = jnp.max(parts[0], axis=0, keepdims=True)
                for x in parts[1:]:
                    m = jnp.maximum(m, jnp.max(x, axis=0, keepdims=True))
                o = None
                for b, x in enumerate(parts):
                    w = jnp.exp2((x - m) * C).astype(BF16)
                    y = nn(ve[:, 256 * b:256 * b + 256], w)
                    o = y if o is None else o + y
                ts = slice(256 * t, 256 * t + 256)
                acc[64 * h:64 * h + 64, ts] = o[64 * e:64 * e + 64]
                other = 64 * (1 - e)
                tot[h, :, ts] = o[other:other + 1]
                top[h, :, ts] = m * C

    def to_group(b, ss, i):
        return copy(kvx.at[b], kvx.at[b], ss, blk_rs.at[b], i, "grp")

    def on_z(i):
        return to_group(g, z_ss.at[i], jnp.where((zh == 0) & (i == 1), g + 12, g + 4 + 4 * i))

    def on_z_pass():
        return to_group(gx, z_ss.at[2], g + 4)

    def on_x(b, i):
        return to_group(b, x_ss.at[b // 4, i - 1], 4 * zh + (gx + i) % 4)

    for p in range(3):
        local_pair(p)

    @pl.when(is_far)
    def _():
        def clear(b):
            kvx[b] = jnp.zeros((128, 128), BF16)
        loop(g + 1, 4 * zh + 4, clear)
        def passing(z):
            b = 4 * z + gx
            arrived(kvx.at[b], blk_rs.at[b])

            @pl.when(zh == 1)
            def _():
                on_z_pass().start()
            for i in range(1, 4):
                on_x(b, i).start()
        @pl.when(zh == 3)
        def _():
            pl.semaphore_wait(go, 1)
            passing(0)

        arrived(f_in, f_rs)
        i, j = iota((128, TOK), 0), iota((128, TOK), 1)
        base = 16 * (i // 4) + i % 4
        keys = onehot(j == base)
        rows = f_in[...].reshape(TOK, 128)
        kvx[g] = nn(keys, rows).astype(BF16)
        qz[...] = nn(onehot(j == base + 4), rows).astype(BF16)

        @pl.when(zh == 2)
        def _():
            pl.semaphore_wait(go, 1)
        for i in range(1, 4):
            @pl.when(gx + i < 4)
            def _():
                on_x(g, i).start()

        @pl.when(zh < 2)
        def _():
            pl.semaphore_wait(barrier, 2)
            for i in range(2):
                on_z(i).start()

        @pl.when(zh == 3)
        def _():
            arrived(g_in, g_rs)
            kvx[g - 4] = nn(keys, g_in[...].reshape(TOK, 128)).astype(BF16)
            for i in range(1, 4):
                on_x(g - 4, i).start()

        loop(jnp.where(zh == 3, 1, 0), jnp.minimum(zh, 2), passing)

    for h in range(HEADS):
        spread[h] = onehot(iota((128, TOK), 1) - 8 * (iota((128, TOK), 0) % 64) == off_ref[0, h])

    @pl.when(is_near)
    def _():
        inner = iota((256, 256), 0) // 64 < iota((256, 256), 1) // 64 + core
        for t in range(4):
            arrived(n_in.at[pl.ds(4 * t, 4)], n_rs.at[t])
            arrived(o_in.at[pl.ds(4 * t, 4)], o_rs.at[t])

            def part(b, side):
                x = n_in[4 * b:4 * b + 4, 0:64, :] if side == 0 else o_in[4 * b:4 * b + 4]
                return x.reshape(256, 128)

            for side in range(2):
                x = nt(eye, part(t, side))
                kvt[2 * t + side] = jnp.where(row_one, 1.0, x).astype(BF16)
            asks = []
            for i in range(4 * t, 4 * t + 4):
                x = n_in[i, 64:96, :].astype(F32)
                asks += [jnp.where(low, x, 0.0), jnp.where(low, turn(x), 0.0)]
            qt = jnp.concatenate(asks, axis=0).astype(BF16)
            m = None
            for n in range(2 * t + 2):
                x = nt(part(n // 2, n % 2), qt)
                if n // 2 == t:
                    x = jnp.where(causal if n % 2 == 0 else inner, x, NEG)
                scr[n] = x
                y = jnp.max(x, axis=0, keepdims=True)
                m = y if m is None else jnp.maximum(m, y)
            o = None
            for n in range(2 * t + 2):
                w = jnp.exp2((scr[n] - m) * C).astype(BF16)
                y = nn(kvt[n], w)
                o = y if o is None else o + y
            total = o[0:1]
            norm = o[64:128] / total
            lses = three(m * C + jnp.log(total) * math.log2(math.e))
            for jj in range(4):
                j = 4 * t + jj
                cols = slice(128 * (jj // 2), 128 * (jj // 2) + 128)
                top_half, bottom = norm[0:32, cols], norm[32:64, cols]
                ls = [x[:, cols] for x in lses]
                if jj % 2 == 0:
                    packed = jnp.where(low, top_half, turn(bottom))
                else:
                    packed = jnp.where(low, turn(top_half), bottom)
                tail = jnp.where(row16 == 0, ls[0], jnp.where(row16 == 1, ls[1], jnp.where(row16 == 2, ls[2], 0.0)))
                if jj % 2 == 1:
                    tail = turn(tail)
                ret_send[j, 0:32, :] = packed.astype(BF16)
                ret_send[j, 32:48, :] = tail.astype(BF16)
                send(ret_send.at[j], ret_in.at[head], ret_ss.at[0], ret_rs.at[head], 2 * j + core)

    @pl.when(is_far)
    def _():
        qf = qz[...]
        limit = iota((TOK, 128), 1) - iota((TOK, 128), 0)
        far_m[...] = jnp.full((1, 128), NEG, F32)
        far_o[...] = jnp.zeros((128, 128), F32)

        def slab(n):
            z = jnp.where(zh > 1, jnp.where(n == 0, 0, zh - n + 1), zh - n)

            def wait(b):
                @pl.when(b % 4 != gx)
                def _():
                    arrived(kvx.at[b], blk_rs.at[b])
            loop(4 * z, jnp.minimum(4 * z + 4, g), wait)
            part = kvx[pl.ds(4 * z, 4)].reshape(TOK, 128)
            x = jnp.where(limit >= TOK * z - 128 * g, nt(part, qf), NEG)
            old = far_m[...]
            new = jnp.maximum(old, jnp.max(x, axis=0, keepdims=True))
            xt = jnp.where(row_v, 1.0, nt(eye, part)).astype(BF16)
            y = nn(xt, jnp.exp2((x - new) * C).astype(BF16))
            far_o[...] = far_o[...] * jnp.exp2((old - new) * C) + y
            far_m[...] = new
        loop(0, zh + 1, slab)
        m, o = far_m[...], far_o[...]
        total = o[0:1]
        norm = (o[64:128] / total).astype(BF16)
        ls = three(m * C + jnp.log(total) * math.log2(math.e))
        r = iota((64, 128), 0)
        tail = jnp.where(r == 0, ls[0], jnp.where(r == 1, ls[1], jnp.where(r == 2, ls[2], 0.0)))
        both = jnp.concatenate([norm, tail.astype(BF16)], axis=0)
        i, j = iota((TOK, 128), 0), iota((TOK, 128), 1)
        place = onehot((j == 4 * (i // 16) + i % 16) & (i % 16 < 4))
        fret_send[...] = nt(place, both).astype(BF16).reshape(SEQ, 16, 128)
        loop(0, SEQ, lambda i: send(fret_send.at[i], fret_in.at[head], ret_ss.at[1], fret_rs.at[head], i))

    tok = iota((1, TOK), 1)
    low48 = iota((48, 128), 1) < HD
    zero = jnp.zeros((), BF16)
    for h in range(HEADS):
        arrived(ret_in.at[h], ret_rs.at[h])
        x = ret_in[h]
        left = jnp.concatenate([jnp.where(low48, x, zero), jnp.where(low, zero, x[0:32])], axis=0)
        u = nn(left, spread[h])
        l1 = jnp.where(tok % 8 == off_ref[0, h], u[32:33] + u[33:34] + u[34:35], NEG)
        m0 = top[h]
        big = jnp.maximum(m0, l1)
        w0, w1 = jnp.exp2(m0 - big), jnp.exp2(l1 - big)
        top[h] = big
        tot[h] = w0 * tot[h] + w1
        for a in range(2):
            rows = slice(64 * h + 32 * a, 64 * h + 32 * a + 32)
            acc[rows, :] = acc[rows, :] * w0 + u[48 * a:48 * a + 32] * w1
    for h in range(HEADS):
        arrived(fret_in.at[h], fret_rs.at[h])
        w = tn(fret_in[h], far_hot[h])
        l2 = jnp.where(tok % 128 == off_ref[1, h], w[64:65] + w[65:66] + w[66:67], NEG)
        m0 = top[h]
        big = jnp.maximum(m0, l2)
        w0, w2 = jnp.exp2(m0 - big), jnp.exp2(l2 - big)
        inv = 1.0 / (w0 * tot[h] + w2)
        rows = slice(64 * h, 64 * h + 64)
        out_ref[rows, :] = (acc[rows, :] * (w0 * inv) + w[0:64] * (w2 * inv)).astype(BF16)

    sent(n_send.at[:, pl.ds(0, 64)], out_ss.at[2])

    @pl.when(zh == 2)
    def _():
        sent(f_send, out_ss.at[3])

    @pl.when(is_near)
    def _():
        sent(n_send.at[pl.ds(0, HEADS - 1)], out_ss.at[1])
        sent(ret_send.at[pl.ds(0, 15)], ret_ss.at[0])

    @pl.when(jnp.logical_not(is_near))
    def _():
        sent(n_send, out_ss.at[1])

    @pl.when(is_far)
    def _():
        sent(f_send.at[pl.ds(0, HEADS - 1)], out_ss.at[0])
        sent(fret_send.at[pl.ds(0, SEQ - 1)], ret_ss.at[1])
        for i in range(1, 4):
            @pl.when(gx + i < 4)
            def _():
                on_x(g, i).wait_send()

            loop(0, zh, lambda z: on_x(4 * z + gx, i).wait_send())

        @pl.when(zh < 2)
        def _():
            for i in range(2):
                on_z(i).wait_send()

        @pl.when(zh == 1)
        def _():
            on_z_pass().wait_send()

    @pl.when(jnp.logical_not(is_far))
    def _():
        sent(f_send, out_ss.at[0])


def on_device(queries, keys, values, offsets, out_weight):
    hbm = pl.BlockSpec(memory_space=pltpu.HBM)
    vm = pltpu.VMEM
    dma = pltpu.SemaphoreType.DMA
    merged = pl.pallas_call(
        kernel,
        out_shape=jax.ShapeDtypeStruct((HEADS * HD, TOK), BF16),
        in_specs=[hbm, hbm, hbm, hbm],
        out_specs=pl.BlockSpec(memory_space=pltpu.VMEM),
        scratch_shapes=[
            vm((TOK, HEADS * HD), BF16),
            vm((TOK, HEADS * HD), BF16),
            vm((TOK, HEADS * HD), BF16),
            pltpu.SMEM((2, HEADS), jnp.int32),
            vm((HEADS, 96, 128), BF16),
            vm((HEADS, 16, 128), BF16),
            vm((16, 96, 128), BF16),
            vm((16, 64, 128), BF16),
            vm((SEQ, 16, 128), BF16),
            vm((SEQ, 16, 128), BF16),
            vm((128, 128), BF16),
            vm((8, 128, 256), BF16),
            vm((8, 256, 256), F32),
            vm((16, 48, 128), BF16),
            vm((HEADS, 48, 128), BF16),
            vm((GRP, 128, 128), BF16),
            vm((SEQ, 16, 128), BF16),
            vm((HEADS, 16, 128), BF16),
            vm((HEADS * HD, TOK), F32),
            vm((HEADS, 1, TOK), F32),
            vm((HEADS, 1, TOK), F32),
            vm((HEADS, 128, TOK), BF16),
            vm((HEADS, 16, TOK), BF16),
            vm((1, 128), F32),
            vm((128, 128), F32),
            dma((4,)), dma((4,)), dma((4,)), dma((4,)), dma, dma,
            dma((3,)), dma((4, 3)), dma((GRP,)),
            pltpu.SemaphoreType.REGULAR,
            dma((2,)), dma((HEADS,)), dma((HEADS,)),
        ],
        compiler_params=pltpu.CompilerParams(
            collective_id=0, has_side_effects=True, vmem_limit_bytes=55783424
        ),
    )(queries, keys, values, offsets)
    return tn(merged, out_weight).astype(BF16)


def solution(mesh):
    placed = (P(("grp", "seq"), None), P(("grp", "seq"), None), P(("grp", "seq"), None), P(), P())
    return jax.shard_map(
        on_device, mesh=mesh, in_specs=placed, out_specs=P(("grp", "seq"), None), check_vma=False
    )
```
